32 devices in a mesh: dp: 8 (over z, y), tensor: 4 (over x, core).
Axes of the slice: x: 2, y: 2, z: 4, core: 2. Of those that a mesh axis runs over, the one named last changes fastest.
Arguments:
- lang_in: bfloat16 [3840, 768], P(('dp', 'tensor')), may hold values from -6 to 6
- visn_in: bfloat16 [6912, 768], P(('dp', 'tensor')), may hold values from -6 to 6
- word_len: int32 [192], P(('dp', 'tensor')), may hold values from 5 to 20, as said below
- lang_cot: bfloat16 [3840, 768], P(('dp', 'tensor')), may hold values from -6 to 6
- visn_cot: bfloat16 [6912, 768], P(('dp', 'tensor')), may hold values from -6 to 6
- att_in: float32 [3, 768, 3, 768], P(None, 'dp', None, 'tensor'), may hold values from -0.21875 to 0.21875
- att_out: float32 [3, 768, 768], P(None, 'tensor', 'dp'), may hold values from -0.875 to 0.875
- ffn_up: float32 [2, 768, 3072], P(None, 'dp', 'tensor'), may hold values from -0.21875 to 0.21875
- ffn_down: float32 [2, 3072, 768], P(None, 'tensor', 'dp'), may hold values from -0.109375 to 0.109375
- vectors: float32 [21, 768], replicated, as said below
- ffn_bias1: float32 [2, 3072], replicated, may hold values from -3 to 3
- att_in_m: float32 [3, 768, 3, 768], P(None, 'dp', None, 'tensor'), may hold values from -192 to 192
- att_in_v: float32 [3, 768, 3, 768], P(None, 'dp', None, 'tensor'), may hold values from 967.68 to 3870.72
- att_out_m: float32 [3, 768, 768], P(None, 'tensor', 'dp'), may hold values from -192 to 192
- att_out_v: float32 [3, 768, 768], P(None, 'tensor', 'dp'), may hold values from 967.68 to 3870.72
- ffn_up_m: float32 [2, 768, 3072], P(None, 'dp', 'tensor'), may hold values from -128 to 128
- ffn_up_v: float32 [2, 768, 3072], P(None, 'dp', 'tensor'), may hold values from 430.08 to 1720.32
- ffn_down_m: float32 [2, 3072, 768], P(None, 'tensor', 'dp'), may hold values from -256 to 256
- ffn_down_v: float32 [2, 3072, 768], P(None, 'tensor', 'dp'), may hold values from 1720.32 to 6881.28
- vectors_m: float32 [21, 768], replicated, may hold values from -448 to 448
- vectors_v: float32 [21, 768], replicated, may hold values from 5268.48 to 21073.92
- bias1_m: float32 [2, 3072], replicated, may hold values from -128 to 128
- bias1_v: float32 [2, 3072], replicated, may hold values from 430.08 to 1720.32
Outputs:
- lang_out: float32 [3840, 768], P(('dp', 'tensor'))
- visn_out: float32 [6912, 768], P(('dp', 'tensor'))
- lang_grad: float32 [3840, 768], P(('dp', 'tensor'))
- visn_grad: float32 [6912, 768], P(('dp', 'tensor'))
- att_in_grad: float32 [3, 768, 3, 768], P(None, 'dp', None, 'tensor')
- att_in_m_new: float32 [3, 768, 3, 768], P(None, 'dp', None, 'tensor')
- att_in_v_new: float32 [3, 768, 3, 768], P(None, 'dp', None, 'tensor')
- att_in_new: float32 [3, 768, 3, 768], P(None, 'dp', None, 'tensor')
- att_in_copy: bfloat16 [3, 768, 3, 768], P(None, 'dp', None, 'tensor')
- att_out_grad: float32 [3, 768, 768], P(None, 'tensor', 'dp')
- att_out_m_new: float32 [3, 768, 768], P(None, 'tensor', 'dp')
- att_out_v_new: float32 [3, 768, 768], P(None, 'tensor', 'dp')
- att_out_new: float32 [3, 768, 768], P(None, 'tensor', 'dp')
- att_out_copy: bfloat16 [3, 768, 768], P(None, 'tensor', 'dp')
- ffn_up_grad: float32 [2, 768, 3072], P(None, 'dp', 'tensor')
- ffn_up_m_new: float32 [2, 768, 3072], P(None, 'dp', 'tensor')
- ffn_up_v_new: float32 [2, 768, 3072], P(None, 'dp', 'tensor')
- ffn_up_new: float32 [2, 768, 3072], P(None, 'dp', 'tensor')
- ffn_up_copy: bfloat16 [2, 768, 3072], P(None, 'dp', 'tensor')
- ffn_down_grad: float32 [2, 3072, 768], P(None, 'tensor', 'dp')
- ffn_down_m_new: float32 [2, 3072, 768], P(None, 'tensor', 'dp')
- ffn_down_v_new: float32 [2, 3072, 768], P(None, 'tensor', 'dp')
- ffn_down_new: float32 [2, 3072, 768], P(None, 'tensor', 'dp')
- ffn_down_copy: bfloat16 [2, 3072, 768], P(None, 'tensor', 'dp')
- vectors_grad: float32 [21, 768], replicated
- vectors_m_new: float32 [21, 768], replicated
- vectors_v_new: float32 [21, 768], replicated
- vectors_new: float32 [21, 768], replicated
- bias1_grad: float32 [2, 3072], replicated
- bias1_m_new: float32 [2, 3072], replicated
- bias1_v_new: float32 [2, 3072], replicated
- bias1_new: float32 [2, 3072], replicated
The draws below stay inside these ranges and needn't reach their ends.
Inputs may be any that keep to these rules, and one draw needn't show every extreme that they name: Each item has 20 word slots, of which the first word_len are words; some item has all 20. `vectors`: rows 3, 8, 13, 16 and 19 are layer norms' gains, positive; the other rows are biases and shifts.
All inputs are finite; a program needn't handle non-finite values.
Results may differ from the reference program's by a relative error of at most 0.033.
Values may be sent and summed in bfloat16 or wider, within the bound.
No kernel may reach another device: no remote copies, remote signals or barrier semaphores. Data moves between devices by JAX's collectives and lax.ppermute only.
A program may use at most 128 MiB of HBM per device.

```python
import functools
import math
import jax
import jax.numpy as jnp
from jax import lax

D = 768
HEADS = 12
HD = 64
FF = 3072
LW = 20
RG = 36
WMIN = 5
STEP = 10
ITEMS = 192


def draw_word_len(key, part):
    key = jax.random.fold_in(key, 11)
    lengths = jax.random.randint(key, (ITEMS,), WMIN, LW + 1, dtype=jnp.int32)
    longest = jax.random.randint(jax.random.fold_in(key, 1), (), 0, ITEMS, dtype=jnp.int32)
    return lengths.at[longest].set(LW)


def draw_vectors(key, part):
    key = jax.random.fold_in(key, 23)
    spread = 0.45 * jax.random.normal(key, (21, D), jnp.float32)
    gains = jnp.exp(jax.random.uniform(jax.random.fold_in(key, 2), (21, D), jnp.float32, -0.5, 0.5))
    number = jnp.arange(21)[:, None]
    is_gain = (number < 15) & (number % 5 == 3) | (number >= 15) & ((number - 15) % 3 == 1)
    return jnp.where(is_gain, gains, spread)


def shard_levels(stream_key, dims, cuts, least, high):
    factor_of, own = 1.0, jax.random.fold_in(stream_key, 6)
    for position, shards_of in cuts:
        steps = jnp.exp(jax.random.uniform(jax.random.fold_in(own, position), (shards_of,), jnp.float32, least / len(cuts), high / len(cuts)))
        factor_of = factor_of * jnp.repeat(steps, dims[position] // shards_of).reshape([-1 if axis == position else 1 for axis in range(len(dims))])
    return factor_of


def gaussian(rng, extent, deviation, most, split=(), kind=jnp.bfloat16):
    array = jax.random.normal(rng, extent, jnp.float32) * deviation
    if len(split) > 0:
        array = shard_levels(rng, extent, split, -0.22, 0.18) * array
    return jnp.clip(array, min=-most, max=most).astype(kind)


def setup_inputs(seed: int = 0) -> dict:
    streams_of = jax.random.split(jax.random.key(seed), 24)
    return {
        "lang_in": gaussian(streams_of[0], (ITEMS * LW, D), 1.0, 6.0, ((0, 32),)),
        "visn_in": gaussian(streams_of[1], (ITEMS * RG, D), 1.0, 6.0, ((0, 32),)),
        "word_len": draw_word_len(jax.random.fold_in(streams_of[23], 71), 0),
        "lang_cot": gaussian(streams_of[3], (ITEMS * LW, D), 1.0, 6.0, ((0, 32),)),
        "visn_cot": gaussian(streams_of[4], (ITEMS * RG, D), 1.0, 6.0, ((0, 32),)),
        "att_in": gaussian(streams_of[5], (3, D, 3, D), D ** -0.5, 0.21875, ((1, 8), (3, 4)), jnp.float32),
        "att_out": gaussian(streams_of[6], (3, D, D), (D // 16) ** -0.5, 0.875, ((1, 4), (2, 8)), jnp.float32),
        "ffn_up": gaussian(streams_of[7], (2, D, FF), D ** -0.5, 0.21875, ((1, 8), (2, 4)), jnp.float32),
        "ffn_down": gaussian(streams_of[8], (2, FF, D), FF ** -0.5, 0.109375, ((1, 4), (2, 8)), jnp.float32),
        "vectors": draw_vectors(jax.random.fold_in(streams_of[23], 71), 0),
        "ffn_bias1": gaussian(streams_of[10], (2, FF), 0.5, 3.0, (), jnp.float32),
        "att_in_m": gaussian(streams_of[11], (3, D, 3, D), (0.3 * (ITEMS * (LW + RG)) ** 0.5), 192.0, ((1, 8), (3, 4)), jnp.float32),
        "att_in_v": jnp.clip(jnp.exp(math.log(3870.72) - 1.3862944 * jax.random.uniform(streams_of[12], (3, D, 3, D), jnp.float32) ** shard_levels(streams_of[12], (3, D, 3, D), ((1, 8), (3, 4)), -0.2, 0.2)), 967.68, 3870.72),
        "att_out_m": gaussian(streams_of[13], (3, D, D), (0.3 * (ITEMS * (LW + RG)) ** 0.5), 192.0, ((1, 4), (2, 8)), jnp.float32),
        "att_out_v": jnp.clip(jnp.exp(math.log(3870.72) - 1.3862944 * jax.random.uniform(streams_of[14], (3, D, D), jnp.float32) ** shard_levels(streams_of[14], (3, D, D), ((1, 4), (2, 8)), -0.2, 0.2)), 967.68, 3870.72),
        "ffn_up_m": gaussian(streams_of[15], (2, D, FF), (0.2 * (ITEMS * (LW + RG)) ** 0.5), 128.0, ((1, 8), (2, 4)), jnp.float32),
        "ffn_up_v": jnp.clip(jnp.exp(math.log(1720.32) - 1.3862944 * jax.random.uniform(streams_of[16], (2, D, FF), jnp.float32) ** shard_levels(streams_of[16], (2, D, FF), ((1, 8), (2, 4)), -0.2, 0.2)), 430.08, 1720.32),
        "ffn_down_m": gaussian(streams_of[17], (2, FF, D), (0.4 * (ITEMS * (LW + RG)) ** 0.5), 256.0, ((1, 4), (2, 8)), jnp.float32),
        "ffn_down_v": jnp.clip(jnp.exp(math.log(6881.28) - 1.3862944 * jax.random.uniform(streams_of[18], (2, FF, D), jnp.float32) ** shard_levels(streams_of[18], (2, FF, D), ((1, 4), (2, 8)), -0.2, 0.2)), 1720.32, 6881.28),
        "vectors_m": gaussian(streams_of[19], (21, D), (0.7 * (ITEMS * (LW + RG)) ** 0.5), 448.0, (), jnp.float32),
        "vectors_v": jnp.clip(jnp.exp(jax.random.uniform(streams_of[20], (21, D), jnp.float32, math.log(5268.48), math.log(21073.92))), 5268.48, 21073.92),
        "bias1_m": gaussian(streams_of[21], (2, FF), (0.2 * (ITEMS * (LW + RG)) ** 0.5), 128.0, (), jnp.float32),
        "bias1_v": jnp.clip(jnp.exp(jax.random.uniform(streams_of[22], (2, FF), jnp.float32, math.log(430.08), math.log(1720.32))), 430.08, 1720.32),
    }


@jax.custom_vjp
def low(v):
    return lax.optimization_barrier(v.astype(jnp.bfloat16)).astype(jnp.float32)

@jax.custom_vjp
def low_back(v):
    return v

def low_keep(v):
    return (low(v), None)

def low_pass(kept, grad):
    return (grad,)

def back_keep(v):
    return (v, None)

def back_low(kept, grad):
    return (low(grad),)
low.defvjp(low_keep, low_pass)
low_back.defvjp(back_keep, back_low)
lnorm_eps = 1e-12
decay_one = 0.5
decay_two = 0.5
adam_eps = 1e-08
weight_decay = 0.01
rate_in = 0.03
rate_out = 0.1
rate_up = 0.03
rate_down = 0.015
rate_vector = 0.2
rate_bias = 0.2

def matmul(left, right):
    return jnp.dot(left, right, precision=lax.Precision.HIGHEST, preferred_element_type=jnp.float32)

def layer_norm(summed, gain, shift):
    centre = lax.optimization_barrier(jnp.mean(summed, axis=-1, keepdims=True))
    centered = summed - centre
    spread = lax.optimization_barrier(jnp.mean(centered * centered, axis=-1, keepdims=True))
    return centered * lax.rsqrt(spread + lnorm_eps) * gain + shift

def gelu_exact(inner):
    return 0.5 * inner * (1.0 + lax.erf(inner * 0.7071067811865476))

def adam_step(weight, gradient, first, second, rate):
    first_new = decay_one * first + (1.0 - decay_one) * gradient
    second_new = decay_two * second + (1.0 - decay_two) * gradient * gradient
    fix_one = 1.0 - decay_one ** STEP
    fix_two = 1.0 - decay_two ** STEP
    ratio = first_new / fix_one / (jnp.sqrt(second_new / fix_two) + adam_eps)
    return (first_new, second_new, weight - rate * (ratio + weight_decay * weight))

def project(stream, w_block, vectors, block):
    bias = jnp.stack([vectors[5 * block], jnp.zeros_like(vectors[0]), vectors[5 * block + 1]])
    packed = matmul(low(stream), w_block.reshape(w_block.shape[0], -1))
    return low_back(low(packed.reshape(stream.shape[0], 3, -1) + bias))

def heads(packed, which):
    return packed[:, which].reshape(ITEMS, -1, HEADS, HD)

def attention(queries, key_rows, value_rows, usable):
    factor = HD ** (-0.5)
    scores = low_back(jnp.einsum('bqhd,bkhd->bhqk', queries, key_rows, precision=lax.Precision.HIGHEST) * factor)
    if usable is not None:
        scores = jnp.where(usable[:, None, None, :], scores, -1e+30)
    maxima = lax.optimization_barrier(jnp.max(scores, axis=-1, keepdims=True))
    powers = jnp.exp(scores - maxima)
    weights = low(powers / lax.optimization_barrier(jnp.sum(powers, axis=-1, keepdims=True)))
    mixed = jnp.einsum('bhqk,bkhd->bqhd', weights, value_rows, precision=lax.Precision.HIGHEST)
    return low_back(low(mixed)).reshape(-1, HEADS * HD)

def forward(usable, lang, visn, att_in, att_out, ffn_up, ffn_down, vectors, ffn_bias1):
    w_in = low(att_in)
    w_out = low(att_out)
    w_up = low(ffn_up)
    w_down = low(ffn_down)
    qkv_lang = project(lang, w_in[0], vectors, 0)
    qkv_visn = project(visn, w_in[0], vectors, 0)
    mix_lang = attention(heads(qkv_lang, 0), heads(qkv_visn, 1), heads(qkv_visn, 2), None)
    mix_visn = attention(heads(qkv_visn, 0), heads(qkv_lang, 1), heads(qkv_lang, 2), usable)
    lang_first = layer_norm(lang + low_back(matmul(mix_lang, w_out[0])) + vectors[2], vectors[3], vectors[4])
    visn_first = layer_norm(visn + low_back(matmul(mix_visn, w_out[0])) + vectors[2], vectors[3], vectors[4])

    def self_block(stream, block, mask):
        qkv = project(stream, w_in[block], vectors, block)
        mixed = attention(heads(qkv, 0), heads(qkv, 1), heads(qkv, 2), mask)
        base = 5 * block + 2
        branch = low_back(matmul(mixed, w_out[block]))
        return layer_norm(stream + branch + vectors[base], vectors[base + 1], vectors[base + 2])

    def feed_block(stream, which):
        base = 15 + 3 * which
        inner = low_back(matmul(low(stream), w_up[which]) + ffn_bias1[which])
        active = low(gelu_exact(inner))
        branch = low_back(matmul(active, w_down[which]))
        return layer_norm(stream + branch + vectors[base], vectors[base + 1], vectors[base + 2])
    lang_second = self_block(lang_first, 1, usable)
    visn_second = self_block(visn_first, 2, None)
    return (feed_block(lang_second, 0), feed_block(visn_second, 1))

def reference(lang_in, visn_in, word_len, lang_cot, visn_cot, att_in, att_out, ffn_up, ffn_down, vectors, ffn_bias1, att_in_m, att_in_v, att_out_m, att_out_v, ffn_up_m, ffn_up_v, ffn_down_m, ffn_down_v, vectors_m, vectors_v, bias1_m, bias1_v):
    usable = jnp.arange(LW, dtype=jnp.int32)[None, :] < word_len[:, None]
    outputs, back = jax.vjp(functools.partial(forward, usable), lang_in.astype(jnp.float32), visn_in.astype(jnp.float32), att_in, att_out, ffn_up, ffn_down, vectors, ffn_bias1)
    lang_out, visn_out = outputs
    grads = back((lang_cot.astype(jnp.float32), visn_cot.astype(jnp.float32)))
    in_first, in_second, in_new = adam_step(att_in, grads[2], att_in_m, att_in_v, rate_in)
    out_first, out_second, out_new = adam_step(att_out, grads[3], att_out_m, att_out_v, rate_out)
    up_first, up_second, up_new = adam_step(ffn_up, grads[4], ffn_up_m, ffn_up_v, rate_up)
    down_first, down_second, down_new = adam_step(ffn_down, grads[5], ffn_down_m, ffn_down_v, rate_down)
    vec_first, vec_second, vec_new = adam_step(vectors, grads[6], vectors_m, vectors_v, rate_vector)
    bias_first, bias_second, bias_new = adam_step(ffn_bias1, grads[7], bias1_m, bias1_v, rate_bias)
    return (lang_out, visn_out, grads[0], grads[1], grads[2], in_first, in_second, in_new, in_new.astype(jnp.bfloat16), grads[3], out_first, out_second, out_new, out_new.astype(jnp.bfloat16), grads[4], up_first, up_second, up_new, up_new.astype(jnp.bfloat16), grads[5], down_first, down_second, down_new, down_new.astype(jnp.bfloat16), grads[6], vec_first, vec_second, vec_new, grads[7], bias_first, bias_second, bias_new)
```

```python
import functools

import jax
import jax.numpy as jnp
from jax import lax
from jax.experimental import pallas as pl
from jax.experimental.pallas import tpu as pltpu
from jax.sharding import PartitionSpec as P

HD = 64
LW = 20
STEP = 10

lnorm_eps = 1e-12
decay_one = 0.5
decay_two = 0.5
adam_eps = 1e-08
weight_decay = 0.01
rate_in = 0.03
rate_out = 0.1
rate_up = 0.03
rate_down = 0.015
rate_vector = 0.2
rate_bias = 0.2

F32 = jnp.float32
BF16 = jnp.bfloat16
HIGHEST = lax.Precision.HIGHEST

DIGITS = {
    (8, 4): {"z": ("dp", 4, 2), "y": ("dp", 2, 1), "x": ("tensor", 2, 2), "c": ("tensor", 2, 1)},
    (32, 4): {"y": ("dp", 4, 8), "z": ("dp", 4, 2), "c": ("dp", 2, 1), "x": ("tensor", 4, 1)},
}


class Tree:
    def __init__(self, mesh):
        self.sizes = dict(mesh.shape)
        shape = (self.sizes["dp"], self.sizes["tensor"])
        self.digits = DIGITS.get(shape) or {
            "z": ("dp", shape[0], 1), "x": ("tensor", shape[1], 1)
        }
        self.row_names = [n for n in ("c", "y", "z") if n in self.digits and self.digits[n][0] == "dp"]
        self.col_names = [n for n in ("x", "c") if n in self.digits and self.digits[n][0] == "tensor"]

    def order(self, text):
        return [n for n in text if n in self.digits]

    def swap(self, value, name, mask):
        axis, size, stride = self.digits[name]
        perm = [(i, i ^ (mask * stride)) for i in range(self.sizes[axis])]
        return lax.ppermute(value, axis, perm)

    def row_code(self):
        codes = [0]
        for name in self.row_names:
            axis, size, stride = self.digits[name]
            codes = [c ^ (m * stride) for c in codes for m in range(size)]
        return codes

    def gather(self, shard, text):
        state = {0: shard.reshape((1,) * len(self.row_names) + shard.shape)}
        for name in self.order(text):
            axis, size, stride = self.digits[name]
            if axis == "dp":
                at = self.row_names.index(name)
                state = {
                    j: jnp.concatenate([v] + [self.swap(v, name, m) for m in range(1, size)], axis=at)
                    for j, v in state.items()
                }
            else:
                new = dict(state)
                for j, v in state.items():
                    for m in range(1, size):
                        new[j ^ (m * stride)] = self.swap(v, name, m)
                state = new
        return [state[j].reshape(-1, shard.shape[1]) for j in range(self.sizes["tensor"])]

    def scatter(self, pieces, text):
        dims = [self.digits[n][1] for n in self.row_names]
        width = pieces[0].shape[1]
        state = {j: v.reshape(dims + [-1, width]) for j, v in enumerate(pieces)}
        for name in reversed(self.order(text)):
            axis, size, stride = self.digits[name]
            new = {}
            if axis == "dp":
                at = self.row_names.index(name)
                for j, v in state.items():
                    total = lax.slice_in_dim(v, 0, 1, axis=at).astype(F32)
                    for m in range(1, size):
                        total = total + self.swap(lax.slice_in_dim(v, m, m + 1, axis=at), name, m).astype(F32)
                    new[j] = total.astype(BF16)
            else:
                for j in [j for j in state if (j // stride) % size == 0]:
                    total = state[j].astype(F32)
                    for m in range(1, size):
                        total = total + self.swap(state[j ^ (m * stride)], name, m).astype(F32)
                    new[j] = total.astype(BF16)
            state = new
        return state[0].reshape(-1, width)

    def total(self, value):
        for name in self.order("czyx"):
            axis, size, stride = self.digits[name]
            value = sum([self.swap(value, name, m) for m in range(1, size)], value)
        return value


def adam_step(weight, gradient, first, second, rate):
    first_new = decay_one * first + (1.0 - decay_one) * gradient
    second_new = decay_two * second + (1.0 - decay_two) * gradient * gradient
    fix_one = 1.0 - decay_one**STEP
    fix_two = 1.0 - decay_two**STEP
    ratio = first_new / fix_one / (jnp.sqrt(second_new / fix_two) + adam_eps)
    return (first_new, second_new, weight - rate * (ratio + weight_decay * weight))


def mm(left, right):
    return jnp.dot(left, right, preferred_element_type=F32)


def mm_nt(left, right):
    return lax.dot_general(left, right, (((1,), (1,)), ((), ())), preferred_element_type=F32)


def mm_tn(left, right):
    return lax.dot_general(left, right, (((0,), (0,)), ((), ())), preferred_element_type=F32)


def normed(z, gain, shift):
    centered = z - jnp.mean(z, axis=-1, keepdims=True)
    scale = lax.rsqrt(jnp.mean(centered * centered, axis=-1, keepdims=True) + lnorm_eps)
    xhat = centered * scale
    return xhat * gain + shift, xhat, scale


def norm_back(g, xhat, scale, gain, sums_ref):
    gg = g * gain
    g_z = (gg - jnp.mean(gg, axis=-1, keepdims=True) - xhat * jnp.mean(gg * xhat, axis=-1, keepdims=True)) * scale
    sums_ref[...] = jnp.zeros(sums_ref.shape, F32)
    sums_ref[0:1, :] = jnp.sum(g_z, axis=0, keepdims=True)
    sums_ref[1:2, :] = jnp.sum(g * xhat, axis=0, keepdims=True)
    sums_ref[2:3, :] = jnp.sum(g, axis=0, keepdims=True)
    return g_z


def probabilities(q, k, mask):
    s = jnp.where(mask > 0, mm_nt(q, k) * HD ** (-0.5), -1e30)
    e = jnp.exp(s - jnp.max(s, axis=-1, keepdims=True))
    return e / jnp.sum(e, axis=-1, keepdims=True)


def att_fwd_kernel(n, hn, x_ref, mask_ref, bias_ref, vec_ref, *refs):
    w, (out_ref, xhat_ref, scale_ref, qkv_ref, mix_ref) = refs[:n], refs[n:]
    c = hn * HD
    x = x_ref[...]
    x16 = x.astype(BF16)
    z = x + vec_ref[0:1, :]
    rows = x.shape[0]
    lead = mix_ref.shape[2] - c
    for j in range(n):
        qkv = (mm(x16, w[j][...]) + bias_ref[j : j + 1, :]).astype(BF16)
        qkv_ref[j] = qkv
        parts = [jnp.zeros((rows, lead), BF16)]
        for h in range(hn):
            q, k, v = (qkv[:, i * c + h * HD : i * c + (h + 1) * HD] for i in range(3))
            p = probabilities(q, k, mask_ref[...]).astype(BF16)
            parts.append(mm(p, v).astype(BF16))
        mix = jnp.concatenate(parts, axis=1)
        mix_ref[j] = mix
        z = z + mm_nt(mix, w[j][:, 3 * c - lead :])
    out, xhat, scale = normed(z, vec_ref[1:2, :], vec_ref[2:3, :])
    out_ref[...] = out
    xhat_ref[...] = xhat
    scale_ref[...] = jnp.broadcast_to(scale, scale_ref.shape)


def att_bwd_kernel(n, hn, g_ref, x_ref, mask_ref, vec_ref, xhat_ref, scale_ref, qkv_ref, mix_ref, *refs):
    w, (gin_ref, sums_ref, bias_ref), dw = refs[:n], refs[n : n + 3], refs[n + 3 :]
    c = hn * HD
    x16 = x_ref[...].astype(BF16)
    g_z = norm_back(g_ref[...], xhat_ref[...], scale_ref[:, 0:1], vec_ref[1:2, :], sums_ref)
    wide = g_z.astype(BF16)
    rows = g_z.shape[0]
    lead = mix_ref.shape[2] - c
    gin = g_z
    for j in range(n):
        qkv = qkv_ref[j]
        d_mix = mm(wide, w[j][:, 3 * c - lead :]).astype(BF16)
        dq, dk, dv = [], [], []
        for h in range(hn):
            q, k, v = (qkv[:, i * c + h * HD : i * c + (h + 1) * HD] for i in range(3))
            da = d_mix[:, lead + h * HD : lead + (h + 1) * HD]
            p = probabilities(q, k, mask_ref[...])
            dv.append(mm_tn(p.astype(BF16), da).astype(BF16))
            dp = mm_nt(da, v)
            ds = (p * (dp - jnp.sum(p * dp, axis=-1, keepdims=True))).astype(BF16) * HD ** (-0.5)
            dq.append(mm(ds, k).astype(BF16))
            dk.append(mm_tn(ds, q).astype(BF16))
        d_qkv = jnp.concatenate(dq + dk + dv + [jnp.zeros((rows, c), BF16)], axis=1)
        bias_ref[j : j + 1, :] = jnp.sum(d_qkv.astype(F32), axis=0, keepdims=True)
        at = 3 * c - lead
        d_in = mm_tn(x16, d_qkv)
        dw[j][:, :at] = d_in[:, :at].astype(BF16)
        dw[j][:, at:] = (d_in[:, at:] + mm_tn(wide, mix_ref[j])).astype(BF16)
        gin = gin + mm_nt(d_qkv, w[j][...])
    gin_ref[...] = gin


def ffn_fwd_kernel(n, x_ref, cot_ref, bias_ref, vec_ref, *refs):
    up, down = refs[:n], refs[n : 2 * n]
    out_ref, gz_ref, sums_ref, act_ref, slope_ref = refs[2 * n :]
    x = x_ref[...]
    x16 = x.astype(BF16)
    z = x + vec_ref[0:1, :]
    for j in range(n):
        inner = mm(x16, up[j][...]) + bias_ref[j : j + 1, :]
        half = 0.5 * (1.0 + lax.erf(inner * 0.7071067811865476))
        act = (inner * half).astype(BF16)
        slope_ref[j] = half + inner * (0.3989422804014327 * jnp.exp(-0.5 * inner * inner))
        act_ref[j] = act
        z = z + mm_nt(act, down[j][...])
    out, xhat, scale = normed(z, vec_ref[1:2, :], vec_ref[2:3, :])
    out_ref[...] = out
    gz_ref[...] = norm_back(cot_ref[...].astype(F32), xhat, scale, vec_ref[1:2, :], sums_ref)


def ffn_down_kernel(n, gz_ref, act_ref, slope_ref, *refs):
    down, (inner_ref, bias_ref), dw = refs[:n], refs[n : n + 2], refs[n + 2 :]
    wide = gz_ref[...].astype(BF16)
    for j in range(n):
        dw[j][...] = mm_tn(wide, act_ref[j]).astype(BF16)
        d_inner = (mm(wide, down[j][...]) * slope_ref[j]).astype(BF16)
        inner_ref[j] = d_inner
        bias_ref[j : j + 1, :] = jnp.sum(d_inner.astype(F32), axis=0, keepdims=True)


def ffn_up_kernel(n, gz_ref, x_ref, inner_ref, *refs):
    up, (gin_ref,), dw = refs[:n], refs[n : n + 1], refs[n + 1 :]
    x16 = x_ref[...].astype(BF16)
    gin = gz_ref[...]
    for j in range(n):
        d_inner = inner_ref[j]
        dw[j][...] = mm_tn(x16, d_inner).astype(BF16)
        gin = gin + mm_nt(d_inner, up[j][...])
    gin_ref[...] = gin


def call(kernel, args, outs, flops):
    vmem = pl.BlockSpec(memory_space=pltpu.VMEM)
    moved = sum(a.size * a.dtype.itemsize for a in args) + sum(o.size * o.dtype.itemsize for o in outs)
    return pl.pallas_call(
        kernel,
        out_shape=tuple(outs),
        in_specs=[vmem] * len(args),
        out_specs=tuple([vmem] * len(outs)),
        compiler_params=pltpu.CompilerParams(vmem_limit_bytes=52 * 1024 * 1024),
        cost_estimate=pl.CostEstimate(flops=int(flops), bytes_accessed=int(moved), transcendentals=0),
    )(*args)


def shape(dims, kind=F32):
    return jax.ShapeDtypeStruct(dims, kind)


def att_forward(x, mask, bias, vec, w, hn):
    n, (rows, width) = len(w), x.shape
    mixed = -(-hn * HD // 256) * 256
    outs = [shape((rows, width)), shape((rows, width)), shape((rows, 128)), shape((n, rows, w[0].shape[1]), BF16), shape((n, rows, mixed), BF16)]
    return call(functools.partial(att_fwd_kernel, n, hn), [x, mask, bias, vec] + list(w), outs, 2 * rows * width * width * 4)


def att_backward(g, x, mask, vec, kept, w, hn):
    n, (rows, width) = len(w), x.shape
    outs = [shape((rows, width)), shape((8, width)), shape((n, w[0].shape[1]))] + [shape(w[0].shape, BF16)] * n
    res = call(functools.partial(att_bwd_kernel, n, hn), [g, x, mask, vec] + list(kept) + list(w), outs, 4 * rows * width * width * 4)
    return res[0], res[1], res[2], res[3:]


def ffn_forward(x, cot, bias, vec, up, down):
    n, (rows, width), f = len(up), x.shape, up[0].shape[1]
    outs = [shape((rows, width)), shape((rows, width)), shape((8, width)), shape((n, rows, f), BF16), shape((n, rows, f))]
    return call(functools.partial(ffn_fwd_kernel, n), [x, cot, bias, vec] + list(up) + list(down), outs, 4 * rows * width * f * n)


def ffn_down_back(gz, act, slope, down):
    n, (rows, width), f = len(down), gz.shape, down[0].shape[1]
    outs = [shape((n, rows, f), BF16), shape((n, f))] + [shape(down[0].shape, BF16)] * n
    res = call(functools.partial(ffn_down_kernel, n), [gz, act, slope] + list(down), outs, 4 * rows * width * f * n)
    return res[0], res[1], res[2:]


def ffn_up_back(gz, x, inner, up):
    n, (rows, width), f = len(up), gz.shape, up[0].shape[1]
    outs = [shape((rows, width))] + [shape(up[0].shape, BF16)] * n
    res = call(functools.partial(ffn_up_kernel, n), [gz, x, inner] + list(up), outs, 4 * rows * width * f * n)
    return res[0], res[1:]


def make_local(mesh):
    tree = Tree(mesh)
    n_t = mesh.shape["tensor"]
    orders = {"a0": "zyxc", "a1": "zxyc", "a2": "zyxc", "u0": "zxyc", "d0": "zyxc", "u1": "zxyc", "d1": "xyzc"}

    def local(
        lang_in, visn_in, word_len, lang_cot, visn_cot, att_in, att_out, ffn_up, ffn_down, vectors, ffn_bias1,
        att_in_m, att_in_v, att_out_m, att_out_v, ffn_up_m, ffn_up_v, ffn_down_m, ffn_down_v,
        vectors_m, vectors_v, bias1_m, bias1_v,
    ):
        width = lang_in.shape[1]
        rows = att_in.shape[1]
        cols = att_in.shape[3]
        ff = ffn_up.shape[2]
        heads_here = cols // HD
        items = word_len.shape[0]
        usable = jnp.arange(LW, dtype=jnp.int32)[None, :] < word_len[:, None]
        dp_at, t_at = lax.axis_index("dp"), lax.axis_index("tensor")

        shards = {}
        for b in range(3):
            shards["a%d" % b] = jnp.concatenate(
                [att_in[b].astype(BF16).reshape(rows, 3 * cols), att_out[b].astype(BF16).T], axis=1
            )
        for i in range(2):
            shards["u%d" % i] = ffn_up[i].astype(BF16)
            shards["d%d" % i] = ffn_down[i].astype(BF16).T
        full = {k: tree.gather(v, orders[k]) for k, v in shards.items()}

        blocks = jnp.asarray(tree.row_code(), jnp.int32) ^ dp_at
        index_of = (blocks[:, None] * rows + jnp.arange(rows, dtype=jnp.int32)[None, :]).reshape(-1)
        turn = (jnp.arange(width, dtype=jnp.int32)[:, None] == index_of[None, :])
        turn16, turn32 = turn.astype(BF16), turn.astype(F32)

        def to_rel(value):
            return mm(value, turn16).astype(BF16)

        def to_abs(value):
            return lax.dot_general(value, turn32, (((1,), (1,)), ((), ())), precision=HIGHEST)

        def by_piece(value, axis):
            return jnp.stack([lax.dynamic_index_in_dim(value, t_at ^ j, axis, keepdims=False) for j in range(n_t)], axis=axis)

        vec = jnp.dot(vectors, turn32, precision=HIGHEST)
        vec_heads = by_piece(vectors.reshape(-1, n_t, cols), 1)
        bias_ff = by_piece(ffn_bias1.reshape(2, n_t, ff), 1)

        qv = jnp.zeros((3, n_t, 4 * cols), F32)
        for b in range(3):
            qv = qv.at[b, :, :cols].set(vec_heads[5 * b]).at[b, :, 2 * cols : 3 * cols].set(vec_heads[5 * b + 1])

        def rows3(row):
            return vec[row : row + 3]

        n_lang, n_visn = lang_in.shape[0], visn_in.shape[0]
        slots, regions = n_lang // items, n_visn // items
        item = jnp.concatenate([jnp.arange(n_lang) // slots, jnp.arange(n_visn) // regions])
        is_lang = jnp.arange(n_lang + n_visn) < n_lang
        seen = jnp.concatenate([usable.reshape(-1), jnp.ones((n_visn,), bool)])
        same = (item[:, None] == item[None, :]) & seen[None, :]
        mask0 = (same & (is_lang[:, None] != is_lang[None, :])).astype(F32)
        mask1 = same[:n_lang, :n_lang].astype(F32)
        mask2 = same[n_lang:, n_lang:].astype(F32)

        x0 = to_rel(jnp.concatenate([lang_in, visn_in], axis=0)).astype(F32)
        both1, *kept0 = att_forward(x0, mask0, qv[0], rows3(2), full["a0"], heads_here)
        lang1, visn1 = both1[:n_lang], both1[n_lang:]
        lang2, *kept1 = att_forward(lang1, mask1, qv[1], rows3(7), full["a1"], heads_here)
        visn2, *kept2 = att_forward(visn1, mask2, qv[2], rows3(12), full["a2"], heads_here)
        lang_out, gz_lang, sums15, act0, slope0 = ffn_forward(lang2, to_rel(lang_cot), bias_ff[0], rows3(15), full["u0"], full["d0"])
        visn_out, gz_visn, sums18, act1, slope1 = ffn_forward(visn2, to_rel(visn_cot), bias_ff[1], rows3(18), full["u1"], full["d1"])

        grads = {}
        inner1, bias_visn, dw = ffn_down_back(gz_visn, act1, slope1, full["d1"])
        grads["d1"] = tree.scatter(dw, orders["d1"])
        g_visn, dw = ffn_up_back(gz_visn, visn2, inner1, full["u1"])
        grads["u1"] = tree.scatter(dw, orders["u1"])
        inner0, bias_lang, dw = ffn_down_back(gz_lang, act0, slope0, full["d0"])
        grads["d0"] = tree.scatter(dw, orders["d0"])
        g_lang, dw = ffn_up_back(gz_lang, lang2, inner0, full["u0"])
        grads["u0"] = tree.scatter(dw, orders["u0"])
        g_visn, sums12, bias2, dw = att_backward(g_visn, visn1, mask2, rows3(12), kept2, full["a2"], heads_here)
        grads["a2"] = tree.scatter(dw, orders["a2"])
        g_lang, sums7, bias1, dw = att_backward(g_lang, lang1, mask1, rows3(7), kept1, full["a1"], heads_here)
        grads["a1"] = tree.scatter(dw, orders["a1"])
        g_both, sums2, bias0, dw = att_backward(jnp.concatenate([g_lang, g_visn], axis=0), x0, mask0, rows3(2), kept0, full["a0"], heads_here)
        grads["a0"] = tree.scatter(dw, orders["a0"])

        blank = jnp.zeros((2, width), F32)
        by_rows = to_abs(jnp.concatenate([blank, sums2[:3], blank, sums7[:3], blank, sums12[:3], sums15[:3], sums18[:3]], axis=0))
        hrows = {}
        for b, value in enumerate((bias0, bias1, bias2)):
            hrows[5 * b], hrows[5 * b + 1] = value[:, :cols], value[:, 2 * cols : 3 * cols]
        out_abs = to_abs(jnp.concatenate([lang_out, visn_out, g_both], axis=0))
        n_both = n_lang + n_visn
        lang_out, visn_out = out_abs[:n_lang], out_abs[n_lang:n_both]
        lang_grad, visn_grad = out_abs[n_both : n_both + n_lang], out_abs[n_both + n_lang :]

        for row, value in hrows.items():
            by_rows = by_rows.at[row].set(by_piece(value, 0).reshape(-1))
        bias_all = by_piece(jnp.stack([bias_lang, bias_visn]), 1)
        sums = tree.total(jnp.concatenate([by_rows, bias_all.reshape(-1, width)], axis=0))
        vector_grad, bias1_grad = sums[:21], sums[21:].reshape(ffn_bias1.shape)

        share_in = jnp.stack([grads["a%d" % b][:, : 3 * cols].astype(F32).reshape(rows, 3, cols) for b in range(3)])
        share_out = jnp.stack([grads["a%d" % b][:, 3 * cols :].astype(F32).T for b in range(3)])
        share_up = jnp.stack([grads["u%d" % i].astype(F32) for i in range(2)])
        share_down = jnp.stack([grads["d%d" % i].astype(F32).T for i in range(2)])
        result = [lang_out, visn_out, lang_grad, visn_grad]
        for share, weight, first, second, rate in (
            (share_in, att_in, att_in_m, att_in_v, rate_in),
            (share_out, att_out, att_out_m, att_out_v, rate_out),
            (share_up, ffn_up, ffn_up_m, ffn_up_v, rate_up),
            (share_down, ffn_down, ffn_down_m, ffn_down_v, rate_down),
        ):
            m_new, v_new, w_new = adam_step(weight, share, first, second, rate)
            result += [share, m_new, v_new, w_new, w_new.astype(BF16)]
        for share, weight, first, second, rate in (
            (vector_grad, vectors, vectors_m, vectors_v, rate_vector),
            (bias1_grad, ffn_bias1, bias1_m, bias1_v, rate_bias),
        ):
            m_new, v_new, w_new = adam_step(weight, share, first, second, rate)
            result += [share, m_new, v_new, w_new]
        return tuple(result)

    return local


def solution(mesh):
    rows = P(("dp", "tensor"), None)
    w_in, w_out, w_up, w_down = P(None, "dp", None, "tensor"), P(None, "tensor", "dp"), P(None, "dp", "tensor"), P(None, "tensor", "dp")
    return jax.shard_map(
        make_local(mesh),
        mesh=mesh,
        in_specs=(rows, rows, P(("dp", "tensor")), rows, rows, w_in, w_out, w_up, w_down, P(), P())
        + (w_in,) * 2 + (w_out,) * 2 + (w_up,) * 2 + (w_down,) * 2 + (P(),) * 4,
        out_specs=(rows,) * 4 + (w_in,) * 5 + (w_out,) * 5 + (w_up,) * 5 + (w_down,) * 5 + (P(),) * 8,
        check_vma=False,
    )
```

```python
import functools

import jax
import jax.numpy as jnp
from jax import lax
from jax.experimental import pallas as pl
from jax.experimental.pallas import tpu as pltpu
from jax.sharding import PartitionSpec as P

HD = 64
LW = 20
STEP = 10

lnorm_eps = 1e-12
decay_one = 0.5
decay_two = 0.5
adam_eps = 1e-08
weight_decay = 0.01
rate_in = 0.03
rate_out = 0.1
rate_up = 0.03
rate_down = 0.015
rate_vector = 0.2
rate_bias = 0.2

F32 = jnp.float32
BF16 = jnp.bfloat16
HIGHEST = lax.Precision.HIGHEST

def tie(value, after):
    return lax.optimization_barrier((value, after))[0]


class Plain:
    def __init__(self, mesh):
        self.n_dp, self.n_t = mesh.shape["dp"], mesh.shape["tensor"]
        self.groups = 1

    def row_blocks(self):
        return jnp.arange(self.n_dp, dtype=jnp.int32)

    def piece_at(self, j):
        return jnp.int32(j)

    def gather(self, shard):
        whole = lax.all_gather(shard, "dp", axis=0)[:, None]
        for_all = lax.all_gather(whole, "tensor", axis=0)
        return [[(for_all[j], 0)] for j in range(self.n_t)]

    def first(self, shards):
        return {"a0": self.gather(shards["a0"])}

    def begin(self, pair, shards, after):
        return {name: self.gather(shards[name]) for name in pair}

    def begun(self, state):
        return ()

    def complete(self, state, after):
        return state

    def swap_out(self, stash):
        return list(stash)

    def fold(self, items, after=()):
        stashes, kinds = weight_kinds(items)
        outs = [shape((self.n_t, stashes[0].shape[2], stashes[0].shape[2]), BF16)] * len(items)
        return small(functools.partial(grad_plain_kernel, kinds, self.n_t), stashes, outs, 8, 40, after)

    def send(self, state):
        return state

    def bump(self, state, after=()):
        return state

    def merge(self, state, after=()):
        return state

    def close(self, state):
        out = []
        for full in state:
            mine = lax.psum_scatter(full, "tensor", scatter_dimension=0)
            out.append(lax.psum_scatter(mine, "dp", scatter_dimension=0, tiled=True))
        return out

    def gate(self, state):
        return []

    def first_totals(self, value):
        return lax.psum(value, ("dp", "tensor"))

    def next_total(self, value, axis, after):
        return value


class Grid:
    def __init__(self, mesh):
        self.n_dp, self.n_t = mesh.shape["dp"], mesh.shape["tensor"]
        self.groups = 2
        self.z_groups = [[z * 2 + y for z in range(4)] for y in range(2)]

    def row_blocks(self):
        y = lax.axis_index("dp") % 2
        return jnp.stack([2 * z + (y ^ k) for k in range(2) for z in range(4)])

    def piece_at(self, j):
        return lax.axis_index("tensor") ^ j

    def swap(self, value, axis, mask):
        size = self.n_dp if axis == "dp" else self.n_t
        return lax.ppermute(value, axis, [(i, i ^ mask) for i in range(size)])

    def over_x(self, value):
        return self.swap(value, "tensor", 2)

    def over_core(self, value):
        return self.swap(value, "tensor", 1)

    def over_y(self, value):
        return self.swap(value, "dp", 1)

    def z_gather(self, value):
        z = lax.axis_index("dp") // 2
        out = jnp.zeros((4,) + value.shape, value.dtype)
        out = lax.dynamic_update_slice_in_dim(out, value[None], z, 0)
        for m in range(1, 4):
            out = lax.dynamic_update_slice_in_dim(out, self.swap(value, "dp", 2 * m)[None], z ^ m, 0)
        return out

    def z_scatter(self, value):
        z = lax.axis_index("dp") // 2
        total = lax.dynamic_index_in_dim(value, z, 0, keepdims=False).astype(F32)
        for m in range(1, 4):
            part = lax.dynamic_index_in_dim(value, z ^ m, 0, keepdims=False)
            total = total + self.swap(part, "dp", 2 * m).astype(F32)
        return total.astype(BF16)

    def first(self, shards):
        s = self.z_gather(shards["a0"][None])
        u, t = self.over_x(s), self.over_y(s)
        half = s.shape[-1] // 2
        v = jnp.concatenate([self.over_x(t[..., :half]), self.over_y(u[..., half:])], axis=-1)
        mine = (s, t, u, v)
        other = [self.over_core(k) for k in mine]
        return {"a0": [[(k[0], 0), (k[1], 0)] if j < 2 else [(k[2], 0), (k[3], 0)] for j, k in enumerate((mine, other, mine, other))]}

    def begin(self, pair, shards, after):
        s = lax.all_gather(jnp.stack([shards[n] for n in pair]), "dp", axis=0, axis_index_groups=self.z_groups)
        s = tie(s, after)
        return pair, s, self.over_x(s), self.over_y(s)

    def begun(self, state):
        return state[3:]

    def complete(self, state, after):
        pair, s, u, t = state
        cut_t, cut_u = tie((t, u), after)
        v0, v1 = self.over_x(cut_t[:, 0:1]), self.over_y(cut_u[:, 1:2])
        mine = (s, t, u, v0, v1)
        other = [self.over_core(k) for k in mine]
        out = {}
        for m, name in enumerate(pair):
            out[name] = [
                [(k[0], m), (k[1], m)] if j < 2 else [(k[2], m), (k[3 + m], 0)] for j, k in enumerate((mine, other, mine, other))
            ]
        return out

    def swap_out(self, stash):
        keep, send = stash
        return [keep, self.over_core(send)]

    def fold(self, items, after=()):
        stashes, kinds = weight_kinds(items)
        n, cols = len(items), stashes[0].shape[2]
        half = cols // 2
        cut = cols if n == 2 else cols // 2
        outs = (shape((n, half, cols), BF16),) * 3 + (shape((half, cut), BF16),) * 2
        s, t, u, va, vb = small(functools.partial(grad_kernel, kinds, 2), stashes, outs, 7, 30, after)
        return s, t, u, va, vb

    def send(self, state):
        s, t, u, va, vb = state
        return s, t, u, self.over_x(va), self.over_y(vb)

    def bump(self, state, after=()):
        s, t, u, ra, rb = state
        t, u = tie((t, u), after)
        t, u = small(bump_kernel, [t, u, ra, rb], (shape(t.shape, BF16), shape(u.shape, BF16)), 1.5)
        return s, self.over_y(t), self.over_x(u), t

    def merge(self, state, after=()):
        s, rt, ru, _ = state
        s = tie(s, after)
        n, half, cols = s.shape
        (both,) = small(close_kernel, [s, rt, ru], (shape((4, n, half // 4, cols), BF16),), 1.5)
        return both

    def close(self, both):
        n = both.shape[1]
        if n == 1:
            return [self.z_scatter(both)[0]]
        both = lax.psum_scatter(both, "dp", scatter_dimension=0, axis_index_groups=self.z_groups)
        return [both[i] for i in range(n)]

    def gate(self, state):
        if not isinstance(state, tuple):
            return [state]
        return [state[0] if len(state) == 5 else state[3]]

    def first_totals(self, value):
        for axis, mask in (("tensor", 1), ("dp", 2), ("dp", 4)):
            value = value + self.swap(value, axis, mask)
        return value

    def next_total(self, value, axis, after):
        other = self.over_x(value) if axis == "x" else self.over_y(value)
        return value + tie(other, after)


def adam_step(weight, gradient, first, second, rate):
    first_new = decay_one * first + (1.0 - decay_one) * gradient
    second_new = decay_two * second + (1.0 - decay_two) * gradient * gradient
    fix_one = 1.0 - decay_one**STEP
    fix_two = 1.0 - decay_two**STEP
    ratio = first_new / fix_one / (jnp.sqrt(second_new / fix_two) + adam_eps)
    return (first_new, second_new, weight - rate * (ratio + weight_decay * weight))


def mm(left, right):
    return jnp.dot(left, right, preferred_element_type=F32)


def mm_nt(left, right):
    return lax.dot_general(left, right, (((1,), (1,)), ((), ())), preferred_element_type=F32)


def mm_tn(left, right):
    return lax.dot_general(left, right, (((0,), (0,)), ((), ())), preferred_element_type=F32)


def normed(z, gain, shift):
    centered = z - jnp.mean(z, axis=-1, keepdims=True)
    scale = lax.rsqrt(jnp.mean(centered * centered, axis=-1, keepdims=True) + lnorm_eps)
    xhat = centered * scale
    return xhat * gain + shift, xhat, scale


def norm_back(g, xhat, scale, gain, sums_ref):
    gg = g * gain
    g_z = (gg - jnp.mean(gg, axis=-1, keepdims=True) - xhat * jnp.mean(gg * xhat, axis=-1, keepdims=True)) * scale
    sums_ref[...] = jnp.zeros(sums_ref.shape, F32)
    sums_ref[0:1, :] = jnp.sum(g_z, axis=0, keepdims=True)
    sums_ref[1:2, :] = jnp.sum(g * xhat, axis=0, keepdims=True)
    sums_ref[2:3, :] = jnp.sum(g, axis=0, keepdims=True)
    return g_z


def put_adam(refs, at, gradient, rate):
    w_ref, m_ref, v_ref, g_out, m_out, v_out, w_out, copy_out = refs
    m_new, v_new, w_new = adam_step(w_ref[at], gradient, m_ref[at], v_ref[at], rate)
    g_out[at], m_out[at], v_out[at], w_out[at] = gradient, m_new, v_new, w_new
    copy_out[at] = w_new.astype(BF16)


def adam_ffn_kernel(ins, outs, up_ref, down_ref):
    put_adam(ins[:3] + outs[:5], 0, up_ref[...].astype(F32), rate_up)
    put_adam(ins[3:] + outs[5:], 0, down_ref[...].astype(F32), rate_down)


def adam_att_kernel(ins, outs, share_ref):
    g = share_ref[...].astype(F32)
    cols = ins[0].shape[3]
    for i in range(3):
        put_adam(ins[:3] + outs[:5], (0, i), g[:, i * cols : (i + 1) * cols], rate_in)
    put_adam(ins[3:] + outs[5:], 0, g[:, 3 * cols :].T, rate_out)


def adam_call(kernel, at, shares, groups, earlier):
    flat_in = [a for g in groups for a in g]

    def one(a):
        return pl.BlockSpec((1,) + a.shape[1:], lambda i: at + (0,) * (len(a.shape) - 1))

    outs = []
    for g in groups:
        outs += [shape(g[0].shape)] * 4 + [shape(g[0].shape, BF16)]
    n, n_in, old = len(shares), len(flat_in), list(earlier or ())

    def body(*refs):
        kernel(refs[n : n + n_in], refs[n + n_in + len(old) :], *refs[:n])

    return pl.pallas_call(
        body,
        grid=(1,),
        in_specs=[pl.BlockSpec(a.shape, lambda i: (0, 0)) for a in shares] + [one(a) for a in flat_in] + [pl.BlockSpec(memory_space=pl.ANY)] * len(old),
        out_specs=tuple(one(o) for o in outs),
        out_shape=tuple(outs),
        input_output_aliases={n + n_in + i: i for i in range(len(old))},
        cost_estimate=work(3),
        compiler_params=pltpu.CompilerParams(vmem_limit_bytes=24 * MIB),
    )(*shares, *flat_in, *old)


def head_lanes(hn, width):
    lane = lax.broadcasted_iota(jnp.int32, (1, width), 1) // HD
    return [lane == h for h in range(hn)]


def stacked(value, lanes):
    return jnp.concatenate([jnp.where(m, value, 0.0) for m in lanes], axis=0).astype(BF16)


def gathered(value, lanes):
    rows = value.shape[0] // len(lanes)
    parts = [jnp.where(m, value[h * rows : (h + 1) * rows], 0.0) for h, m in enumerate(lanes)]
    return sum(parts[1:], parts[0])


def probabilities(q_rows, k, mask):
    rows = mask.shape[0]
    s = mm_nt(q_rows, k).reshape(-1, rows, rows) * HD ** (-0.5)
    s = jnp.where(mask[None] > 0, s, -1e30)
    e = jnp.exp(s - jnp.max(s, axis=-1, keepdims=True))
    return (e / jnp.sum(e, axis=-1, keepdims=True)).reshape(-1, rows)


def att_fwd_kernel(n, nw, hn, x_ref, mask_ref, bias_ref, vec_ref, *refs):
    w, (out_ref, xhat_ref, scale_ref, qkv_ref, mix_ref) = split(refs[:nw], n), refs[nw:]
    c, lanes = hn * HD, head_lanes(hn, 256)
    x = x_ref[...]
    x16 = x.astype(BF16)
    z = x + vec_ref[0:1, :]
    for j in range(n):
        qkv = times(x16, w[j]) + bias_ref[j : j + 1, :]
        k = pltpu.roll(qkv[:, c - 64 : c + 192], 192, 1).astype(BF16)
        q, v = qkv[:, :256].astype(BF16), qkv[:, 2 * c : 2 * c + 256].astype(BF16)
        qkv_ref[j, :, :256], qkv_ref[j, :, 256:512], qkv_ref[j, :, 512:] = q, k, v
        p = probabilities(stacked(q.astype(F32), lanes), k, mask_ref[...]).astype(BF16)
        mix = pltpu.roll(gathered(mm(p, v), lanes), 64, 1).astype(BF16)
        mix_ref[j] = mix
        z = z + times_t(mix, w[j], 3 * c - 64)
    out, xhat, scale = normed(z, vec_ref[1:2, :], vec_ref[2:3, :])
    out_ref[...] = out
    xhat_ref[...] = xhat
    scale_ref[...] = jnp.broadcast_to(scale, scale_ref.shape)


def att_bwd_kernel(n, nw, hn, g_ref, x_ref, mask_ref, vec_ref, xhat_ref, scale_ref, qkv_ref, mix_ref, *refs):
    w, (gin_ref, sums_ref, bias_ref), stash = split(refs[:nw], n), refs[nw : nw + 3], refs[nw + 3 :]
    c, lanes, groups = hn * HD, head_lanes(hn, 256), len(stash)
    g_z = norm_back(g_ref[...], xhat_ref[...], scale_ref[:, 0:1], vec_ref[1:2, :], sums_ref)
    wide, x16 = g_z.astype(BF16), x_ref[...].astype(BF16)
    for ref in stash:
        ref[0], ref[1] = x16, wide
    gin = g_z
    for j in range(n):
        q, k, v = qkv_ref[j, :, :256], qkv_ref[j, :, 256:512], qkv_ref[j, :, 512:]
        d_mix = pltpu.roll(times_from(wide, w[j], 3 * c - 64), 192, 1).astype(BF16)
        da, q = stacked(d_mix.astype(F32), lanes), stacked(q.astype(F32), lanes)
        p = probabilities(q, k, mask_ref[...])
        dv = mm_tn(p.astype(BF16), da)
        dp = mm_nt(da, v)
        ds = (p * (dp - jnp.sum(p * dp, axis=-1, keepdims=True))).astype(BF16) * HD ** (-0.5)
        dq = gathered(mm(ds, k), lanes)
        dk = pltpu.roll(mm_tn(ds, q), 64, 1)
        front = [dq[:, :128], dq[:, 128:] + dk[:, :128], dk[:, 128:], dv[:, :128]]
        d_qkv = jnp.concatenate(front + [dv[:, 128:]], axis=1).astype(BF16)
        bias_ref[j : j + 1, :640] = jnp.sum(d_qkv.astype(F32), axis=0, keepdims=True)
        place = stash[j % groups].at[2 + j // groups]
        place[:, :512] = d_qkv[:, :512]
        place[:, 512:640] = d_qkv[:, 512:] + mix_ref[j, :, :128]
        place[:, 640:] = mix_ref[j, :, 128:]
        gin = gin + times_t(d_qkv, w[j], 0, 640)
    gin_ref[...] = gin


def ffn_kernel(n, nw, x_ref, cot_ref, bias_ref, vec_ref, *refs):
    up, down = split(refs[:nw], n), split(refs[nw : 2 * nw], n)
    out_ref, gin_ref, sums_ref, dbias_ref = refs[2 * nw : 2 * nw + 4]
    slope_ref, stash = refs[-1], refs[2 * nw + 4 : -1]
    groups, held = len(stash), n // len(stash)
    x = x_ref[...]
    x16 = x.astype(BF16)
    z = x + vec_ref[0:1, :]
    for j in range(n):
        inner = times(x16, up[j]) + bias_ref[j : j + 1, :]
        half = 0.5 * (1.0 + lax.erf(inner * 0.7071067811865476))
        act = (inner * half).astype(BF16)
        slope_ref[j] = half + inner * (0.3989422804014327 * jnp.exp(-0.5 * inner * inner))
        stash[j % groups][2 + j // groups] = act
        z = z + times_t(act, down[j])
    out, xhat, scale = normed(z, vec_ref[1:2, :], vec_ref[2:3, :])
    out_ref[...] = out
    g_z = norm_back(cot_ref[...].astype(F32), xhat, scale, vec_ref[1:2, :], sums_ref)
    wide = g_z.astype(BF16)
    for ref in stash:
        ref[0], ref[1] = x16, wide
    gin = g_z
    for j in range(n):
        d_inner = (times(wide, down[j]) * slope_ref[j]).astype(BF16)
        dbias_ref[j : j + 1, :] = jnp.sum(d_inner.astype(F32), axis=0, keepdims=True)
        stash[j % groups][2 + held + j // groups] = d_inner
        gin = gin + times_t(d_inner, up[j])
    gin_ref[...] = gin


def weight_grad(kind, refs, i, held):
    total = None
    for ref in refs:
        if kind == "d":
            part = mm_tn(ref[1], ref[2 + i])
        elif kind == "u":
            part = mm_tn(ref[0], ref[2 + held + i])
        else:
            both = ref[2 + i]
            part = mm_tn(ref[0], both)
            tail = mm_tn(ref[1], both[:, 512:])
            own = lax.broadcasted_iota(jnp.int32, (1, 256), 1) < 64
            part = jnp.concatenate([part[:, :512], jnp.where(own, part[:, 512:], tail)], axis=1)
        total = part if total is None else total + part
    return total.astype(BF16)


def grad_kernel(kinds, held, *refs):
    outs = refs[-5:]
    s_ref, t_ref, u_ref, va_ref, vb_ref = outs
    for m, (kind, at) in enumerate(kinds):
        g = weight_grad(kind, [refs[i] for i in at], 1, held)
        half = g.shape[0] // 2
        u_ref[m], v = g[:half], g[half:]
        if len(kinds) == 1:
            va_ref[...], vb_ref[...] = v[:, : v.shape[1] // 2], v[:, v.shape[1] // 2 :]
        elif m == 0:
            va_ref[...] = v
        else:
            vb_ref[...] = v
        g = weight_grad(kind, [refs[i] for i in at], 0, held)
        s_ref[m], t_ref[m] = g[:half], g[half:]


def grad_plain_kernel(kinds, held, *refs):
    for m, (kind, at) in enumerate(kinds):
        for i in range(held):
            refs[len(refs) - len(kinds) + m][i] = weight_grad(kind, [refs[k] for k in at], i, held)


def bump_kernel(t_ref, u_ref, a_ref, b_ref, t_out, u_out):
    cut, cols, last = a_ref.shape[1], t_ref.shape[2], u_ref.shape[0] - 1
    t_out[...] = t_ref[...]
    u_out[...] = u_ref[...]
    t_out[0, :, :cut] = (t_ref[0, :, :cut].astype(F32) + a_ref[...].astype(F32)).astype(BF16)
    u_out[last, :, cols - cut :] = (u_ref[last, :, cols - cut :].astype(F32) + b_ref[...].astype(F32)).astype(BF16)


def close_kernel(s_ref, t_ref, u_ref, out_ref):
    n, rows = s_ref.shape[0], s_ref.shape[1] // 4
    for m in range(n):
        for z in range(4):
            at = slice(z * rows, (z + 1) * rows)
            out_ref[z, m] = (s_ref[m, at].astype(F32) + t_ref[m, at].astype(F32) + u_ref[m, at].astype(F32)).astype(BF16)


def small(kernel, args, outs, micros, limit=24, after=()):
    vmem, n_in = pl.BlockSpec(memory_space=pltpu.VMEM), len(args)

    def body(*refs):
        kernel(*refs[:n_in], *refs[n_in + len(after) :])

    return pl.pallas_call(
        body,
        in_specs=[vmem] * n_in + [pl.BlockSpec(memory_space=pl.ANY)] * len(after),
        out_specs=tuple([vmem] * len(outs)),
        out_shape=tuple(outs),
        cost_estimate=work(micros),
        compiler_params=pltpu.CompilerParams(vmem_limit_bytes=limit * MIB),
    )(*args, *after)


def flat(ref):
    k, _, r, c = ref.shape
    return ref[...].reshape(k * r, c)


def times(x, refs):
    total, at = None, 0
    for ref in refs:
        w = flat(ref)
        part = mm(x[:, at : at + w.shape[0]], w)
        total = part if total is None else total + part
        at += w.shape[0]
    return total


def times_t(x, refs, start=0, stop=None):
    return jnp.concatenate([mm_nt(x, flat(ref)[:, start:stop]) for ref in refs], axis=1)


def times_from(x, refs, start):
    total, at = None, 0
    for ref in refs:
        w = flat(ref)[:, start:]
        part = mm(x[:, at : at + w.shape[0]], w)
        total = part if total is None else total + part
        at += w.shape[0]
    return total


def split(refs, n):
    size = len(refs) // n
    return [refs[i * size : (i + 1) * size] for i in range(n)]


MIB = 1024 * 1024


def work(micros):
    return pl.CostEstimate(flops=int(micros * 1.1e9), bytes_accessed=1024, transcendentals=0)


def call(kernel, args, weights, outs, cost, vmem, after=(), scratch=()):
    chunks = [c for piece in weights for c in piece]
    n_in, waits = len(args) + len(chunks), len(after)

    def body(*refs):
        kernel(*refs[:n_in], *refs[n_in + waits :])

    once = pl.Buffered(buffer_count=1)

    def whole(a):
        return pl.BlockSpec(a.shape, lambda i, nd=len(a.shape): (0,) * nd, pipeline_mode=once)

    def picked(a, m):
        k, _, r, c = a.shape
        return pl.BlockSpec((k, 1, r, c), lambda i: (0, m, 0, 0), pipeline_mode=once)

    return pl.pallas_call(
        body,
        grid=(1,),
        out_shape=tuple(outs),
        scratch_shapes=list(scratch),
        in_specs=[whole(a) for a in args] + [picked(a, m) for a, m in chunks]
        + [pl.BlockSpec(memory_space=pl.ANY)] * waits,
        out_specs=tuple(whole(o) for o in outs),
        compiler_params=pltpu.CompilerParams(vmem_limit_bytes=vmem * MIB),
        cost_estimate=cost,
    )(*args, *[a for a, m in chunks], *after)


def shape(dims, kind=F32):
    return jax.ShapeDtypeStruct(dims, kind)


def dims_of(piece):
    return [a.shape[0] * a.shape[2] for a, m in piece], piece[0][0].shape[3]


def count(w):
    return len(w), sum(len(p) for p in w)


def att_forward(x, mask, bias, vec, w, hn):
    (n, nw), (rows, width) = count(w), x.shape
    outs = [shape((rows, width)), shape((rows, width)), shape((rows, 128)), shape((n, rows, 768), BF16), shape((n, rows, 256), BF16)]
    return call(functools.partial(att_fwd_kernel, n, nw, hn), [x, mask, bias, vec], w, outs, work(4 + rows / 50), 30)


def att_backward(g, x, mask, vec, kept, w, hn, groups, after=()):
    (n, nw), (rows, width) = count(w), x.shape
    outs = [shape((rows, width)), shape((8, width)), shape((n, dims_of(w[0])[1]))] + [shape((2 + n // groups, rows, width), BF16)] * groups
    res = call(functools.partial(att_bwd_kernel, n, nw, hn), [g, x, mask, vec] + list(kept), w, outs, work(5 + rows / 30), 30, after)
    return res[0], res[1], res[2], res[3:]


def ffn_both(x, cot, bias, vec, up, down, groups, after=()):
    (n, nw), (rows, width), f = count(up), x.shape, dims_of(up[0])[1]
    outs = [shape((rows, width)), shape((rows, width)), shape((8, width)), shape((n, f))]
    outs += [shape((2 + 2 * n // groups, rows, width), BF16)] * groups
    scratch = [pltpu.VMEM((n, rows, f), F32)]
    res = call(functools.partial(ffn_kernel, n, nw), [x, cot, bias, vec], up + down, outs, work(5 + rows / 30), 38, after, scratch)
    return res[0], res[1], res[2], res[3], res[4:]


def weight_kinds(items):
    stashes = []
    kinds = []
    for kind, arrays in items:
        at = []
        for array in arrays:
            same = [i for i, s in enumerate(stashes) if s is array]
            at.append(same[0] if same else len(stashes))
            stashes += [] if same else [array]
        kinds.append((kind, tuple(at)))
    return stashes, tuple(kinds)


def make_local(mesh):
    n_t = mesh.shape["tensor"]
    net = (Grid if (mesh.shape["dp"], n_t) == (8, 4) else Plain)(mesh)

    def local(
        lang_in, visn_in, word_len, lang_cot, visn_cot, att_in, att_out, ffn_up, ffn_down, vectors, ffn_bias1,
        att_in_m, att_in_v, att_out_m, att_out_v, ffn_up_m, ffn_up_v, ffn_down_m, ffn_down_v,
        vectors_m, vectors_v, bias1_m, bias1_v,
    ):
        width = lang_in.shape[1]
        rows = att_in.shape[1]
        cols = att_in.shape[3]
        ff = ffn_up.shape[2]
        heads_here = cols // HD
        items = word_len.shape[0]
        usable = jnp.arange(LW, dtype=jnp.int32)[None, :] < word_len[:, None]

        shards = {}
        for b in range(3):
            shards["a%d" % b] = jnp.concatenate(
                [att_in[b].astype(BF16).reshape(rows, 3 * cols), att_out[b].astype(BF16).T], axis=1
            )
        for i in range(2):
            shards["u%d" % i] = ffn_up[i].astype(BF16)
            shards["d%d" % i] = ffn_down[i].astype(BF16).T

        index_of = (net.row_blocks()[:, None] * rows + jnp.arange(rows, dtype=jnp.int32)[None, :]).reshape(-1)
        turn = (jnp.arange(width, dtype=jnp.int32)[:, None] == index_of[None, :])
        turn16, turn32 = turn.astype(BF16), turn.astype(F32)

        def to_rel(value):
            return mm(value, turn16).astype(BF16)

        def to_abs(value):
            return lax.dot_general(value, turn32, (((1,), (1,)), ((), ())), precision=HIGHEST)

        def by_piece(value, axis):
            return jnp.stack([lax.dynamic_index_in_dim(value, net.piece_at(j), axis, keepdims=False) for j in range(n_t)], axis=axis)

        vec = jnp.dot(vectors, turn32, precision=HIGHEST)
        vec_heads = by_piece(vectors.reshape(-1, n_t, cols), 1)
        bias_ff = by_piece(ffn_bias1.reshape(2, n_t, ff), 1)

        qv = jnp.zeros((3, n_t, 4 * cols), F32)
        for b in range(3):
            qv = qv.at[b, :, :cols].set(vec_heads[5 * b]).at[b, :, 2 * cols : 3 * cols].set(vec_heads[5 * b + 1])

        def rows3(row):
            return vec[row : row + 3]

        n_lang, n_visn = lang_in.shape[0], visn_in.shape[0]
        slots, regions = n_lang // items, n_visn // items
        item = jnp.concatenate([jnp.arange(n_lang) // slots, jnp.arange(n_visn) // regions])
        is_lang = jnp.arange(n_lang + n_visn) < n_lang
        seen = jnp.concatenate([usable.reshape(-1), jnp.ones((n_visn,), bool)])
        same = (item[:, None] == item[None, :]) & seen[None, :]
        mask0 = (same & (is_lang[:, None] != is_lang[None, :])).astype(F32)
        mask1 = same[:n_lang, :n_lang].astype(F32)
        mask2 = same[n_lang:, n_lang:].astype(F32)

        x0 = to_rel(jnp.concatenate([lang_in, visn_in], axis=0)).astype(F32)
        full = net.first(shards)
        later = tie({k: v for k, v in shards.items() if k != "a0"}, shards["a0"])
        pair1 = net.begin(("a1", "a2"), later, ())
        both1, *kept0 = att_forward(x0, mask0, qv[0], rows3(2), full["a0"], heads_here)
        full.update(net.complete(pair1, both1))
        pair2 = net.begin(("u0", "d0"), later, net.begun(pair1))
        lang1, visn1 = both1[:n_lang], both1[n_lang:]
        lang2, *kept1 = att_forward(lang1, mask1, qv[1], rows3(7), full["a1"], heads_here)
        visn2, *kept2 = att_forward(visn1, mask2, qv[2], rows3(12), full["a2"], heads_here)
        full.update(net.complete(pair2, (lang2, visn2)))
        pair3 = net.begin(("u1", "d1"), later, net.begun(pair2))
        groups = net.groups
        lang_out, g_lang, sums15, bias_lang, stash = ffn_both(lang2, to_rel(lang_cot), bias_ff[0], rows3(15), full["u0"], full["d0"], groups)
        full.update(net.complete(pair3, lang_out))
        rows_f0 = net.swap_out(stash)
        g_lang, sums7, bias1, stash = att_backward(g_lang, lang1, mask1, rows3(7), kept1, full["a1"], heads_here, groups)
        rows_a1 = net.swap_out(stash)
        part0 = net.send(net.fold([("d", rows_f0), ("u", rows_f0)], [sums7]))
        first = ffn_both(visn2, to_rel(visn_cot), bias_ff[1], rows3(18), full["u1"], full["d1"], groups, net.gate(part0))
        part0 = net.bump(part0, first[2])
        visn_out, g_visn, sums18, bias_visn, stash = tie(first, net.gate(part0))
        rows_f1 = net.swap_out(stash)
        g_visn, sums12, bias2, stash = att_backward(g_visn, visn1, mask2, rows3(12), kept2, full["a2"], heads_here, groups, net.gate(part0))
        rows_a2 = net.swap_out(stash)
        part1 = net.send(net.fold([("d", rows_f1), ("u", rows_f1)], [sums12]))
        part2 = net.send(net.fold([("a", rows_a1), ("a", rows_a2)], net.gate(part1)))
        part0 = net.merge(part0, net.gate(part2))
        share0 = net.close(part0)
        first = att_backward(
            jnp.concatenate([g_lang, g_visn], axis=0), x0, mask0, rows3(2), kept0, full["a0"], heads_here, groups, net.gate(part2) + net.gate(part0)
        )
        part1, part2 = net.bump(part1, first[1]), net.bump(part2, first[1])
        g_both, sums2, bias0, stash = tie(first, net.gate(part1) + net.gate(part2))
        rows_a0 = net.swap_out(stash)
        part3 = net.send(net.fold([("a", rows_a0)], net.gate(part2)))
        part1 = net.merge(part1, net.gate(part3))
        share1 = net.close(part1)
        part2 = net.merge(part2, net.gate(part1))
        share2 = net.close(part2)

        t_in, t_in_m, t_in_v = (jnp.transpose(k, (0, 2, 1, 3)) for k in (att_in, att_in_m, att_in_v))
        up_all = (ffn_up, ffn_up_m, ffn_up_v)
        down_all = [jnp.transpose(k, (0, 2, 1)) for k in (ffn_down, ffn_down_m, ffn_down_v)]
        ffn_new = adam_call(adam_ffn_kernel, (0,), share0[1::-1], [up_all, down_all], None)
        ffn_new = adam_call(adam_ffn_kernel, (1,), share1[1::-1], [up_all, down_all], ffn_new)
        blank = jnp.zeros((2, width), F32)
        by_rows = to_abs(jnp.concatenate([blank, sums2[:3], blank, sums7[:3], blank, sums12[:3], sums15[:3], sums18[:3]], axis=0))
        hrows = {}
        for b, value in enumerate((bias0, bias1, bias2)):
            hrows[5 * b], hrows[5 * b + 1] = value[:, :cols], value[:, 2 * cols : 3 * cols]
        out_abs = to_abs(jnp.concatenate([lang_out, visn_out, g_both], axis=0))
        n_both = n_lang + n_visn
        lang_out, visn_out = out_abs[:n_lang], out_abs[n_lang:n_both]
        lang_grad, visn_grad = out_abs[n_both : n_both + n_lang], out_abs[n_both + n_lang :]

        for row, value in hrows.items():
            by_rows = by_rows.at[row].set(by_piece(value, 0).reshape(-1))
        bias_all = by_piece(jnp.stack([bias_lang, bias_visn]), 1)
        sums = net.first_totals(tie(jnp.concatenate([by_rows, bias_all.reshape(-1, width)], axis=0), net.gate(part2)))
        part3 = net.bump(part3)
        sums = net.next_total(sums, "x", net.gate(part3))
        part3 = net.merge(part3, ffn_new[0])
        sums = net.next_total(sums, "y", net.gate(part3))
        share3 = net.close(part3)
        vector_grad, bias1_grad = sums[:21], sums[21:].reshape(ffn_bias1.shape)

        att_all = [(t_in, t_in_m, t_in_v), (att_out, att_out_m, att_out_v)]
        att_new = adam_call(adam_att_kernel, (1,), share2[:1], att_all, None)
        att_new = adam_call(adam_att_kernel, (2,), share2[1:], att_all, att_new)
        att_new = adam_call(adam_att_kernel, (0,), share3, att_all, att_new)
        in_new = [jnp.transpose(k, (0, 2, 1, 3)) for k in att_new[:5]]

        result = [lang_out, visn_out, lang_grad, visn_grad] + in_new + list(att_new[5:]) + list(ffn_new[:5]) + [jnp.transpose(k, (0, 2, 1)) for k in ffn_new[5:]]
        for share, weight, first, second, rate in (
            (vector_grad, vectors, vectors_m, vectors_v, rate_vector),
            (bias1_grad, ffn_bias1, bias1_m, bias1_v, rate_bias),
        ):
            m_new, v_new, w_new = adam_step(weight, share, first, second, rate)
            result += [share, m_new, v_new, w_new]
        return tuple(result)

    return local


def solution(mesh):
    rows = P(("dp", "tensor"), None)
    w_in, w_out, w_up, w_down = P(None, "dp", None, "tensor"), P(None, "tensor", "dp"), P(None, "dp", "tensor"), P(None, "tensor", "dp")
    return jax.shard_map(
        make_local(mesh),
        mesh=mesh,
        in_specs=(rows, rows, P(("dp", "tensor")), rows, rows, w_in, w_out, w_up, w_down, P(), P())
        + (w_in,) * 2 + (w_out,) * 2 + (w_up,) * 2 + (w_down,) * 2 + (P(),) * 4,
        out_specs=(rows,) * 4 + (w_in,) * 5 + (w_out,) * 5 + (w_up,) * 5 + (w_down,) * 5 + (P(),) * 8,
        check_vma=False,
    )
```

```python
import functools

import jax
import jax.numpy as jnp
from jax import lax
from jax.experimental import pallas as pl
from jax.experimental.pallas import tpu as pltpu
from jax.sharding import PartitionSpec as P

HD = 64
LW = 20
STEP = 10

lnorm_eps = 1e-12
decay_one = 0.5
decay_two = 0.5
adam_eps = 1e-08
weight_decay = 0.01
rate_in = 0.03
rate_out = 0.1
rate_up = 0.03
rate_down = 0.015
rate_vector = 0.2
rate_bias = 0.2

F32 = jnp.float32
BF16 = jnp.bfloat16
HIGHEST = lax.Precision.HIGHEST

def tie(value, after):
    return lax.optimization_barrier((value, after))[0]


class Plain:
    def __init__(self, mesh):
        self.n_dp, self.n_t = mesh.shape["dp"], mesh.shape["tensor"]
        self.groups = 1

    def row_blocks(self):
        return jnp.arange(self.n_dp, dtype=jnp.int32)

    def piece_at(self, j):
        return jnp.int32(j)

    def gather(self, shard):
        whole = lax.all_gather(shard, "dp", axis=0)[:, None]
        for_all = lax.all_gather(whole, "tensor", axis=0)
        return [[(for_all[j], 0)] for j in range(self.n_t)]

    def first(self, shards):
        return {"a0": self.gather(shards["a0"])}

    def begin(self, pair, shards, after):
        return {name: self.gather(shards[name]) for name in pair}

    def begin_late(self, pair, shards):
        return self.begin(pair, shards, ())

    def gather_late(self, state, after):
        return state

    def complete_late(self, state, after):
        return state

    def swap_late(self, state, after):
        return state

    def begun(self, state):
        return ()

    def complete(self, state, after):
        return state

    def swap_out(self, stash):
        return list(stash)

    def fold(self, items, after=()):
        stashes, kinds = weight_kinds(items)
        outs = [shape((self.n_t, stashes[0].shape[2], stashes[0].shape[2]), BF16)] * len(items)
        return small(functools.partial(grad_plain_kernel, kinds, self.n_t), stashes, outs, 8, 40, after)

    def send(self, state, after=()):
        return state

    def bump(self, *states, after=()):
        return list(states)

    def merge_and_bump(self, state, *others, after=()):
        return [state, *others]

    def go(self, state, after=()):
        return state

    def landed(self, state):
        return ()

    def merge(self, state, after=()):
        return state

    def close(self, state):
        out = []
        for full in state:
            mine = lax.psum_scatter(full, "tensor", scatter_dimension=0)
            out.append(lax.psum_scatter(mine, "dp", scatter_dimension=0, tiled=True))
        return out

    def gate(self, state):
        return []

    def first_totals(self, value):
        return lax.psum(value, ("dp", "tensor"))

    def next_total(self, value, axis, after):
        return value


class Grid:
    def __init__(self, mesh):
        self.n_dp, self.n_t = mesh.shape["dp"], mesh.shape["tensor"]
        self.groups = 2
        self.z_groups = [[z * 2 + y for z in range(4)] for y in range(2)]

    def row_blocks(self):
        y = lax.axis_index("dp") % 2
        return jnp.stack([2 * z + (y ^ k) for k in range(2) for z in range(4)])

    def piece_at(self, j):
        return lax.axis_index("tensor") ^ j

    def swap(self, value, axis, mask):
        size = self.n_dp if axis == "dp" else self.n_t
        return lax.ppermute(value, axis, [(i, i ^ mask) for i in range(size)])

    def over_x(self, value):
        return self.swap(value, "tensor", 2)

    def over_core(self, value):
        return self.swap(value, "tensor", 1)

    def over_y(self, value):
        return self.swap(value, "dp", 1)

    def z_gather(self, value):
        z = lax.axis_index("dp") // 2
        out = jnp.zeros((4,) + value.shape, value.dtype)
        out = lax.dynamic_update_slice_in_dim(out, value[None], z, 0)
        for m in range(1, 4):
            out = lax.dynamic_update_slice_in_dim(out, self.swap(value, "dp", 2 * m)[None], z ^ m, 0)
        return out

    def z_scatter(self, value):
        z = lax.axis_index("dp") // 2
        total = lax.dynamic_index_in_dim(value, z, 0, keepdims=False).astype(F32)
        for m in range(1, 4):
            part = lax.dynamic_index_in_dim(value, z ^ m, 0, keepdims=False)
            total = total + self.swap(part, "dp", 2 * m).astype(F32)
        return total.astype(BF16)

    def first(self, shards):
        s = self.z_gather(shards["a0"][None])
        u, t = self.over_x(s), self.over_y(s)
        half = s.shape[-1] // 2
        v = jnp.concatenate([self.over_x(t[..., :half]), self.over_y(u[..., half:])], axis=-1)
        mine = (s, t, u, v)
        other = [self.over_core(k) for k in mine]
        return {"a0": [[(k[0], 0), (k[1], 0)] if j < 2 else [(k[2], 0), (k[3], 0)] for j, k in enumerate((mine, other, mine, other))]}

    def begin(self, pair, shards, after):
        s = lax.all_gather(jnp.stack([shards[n] for n in pair]), "dp", axis=0, axis_index_groups=self.z_groups)
        s = tie(s, after)
        return pair, s, self.over_x(s), self.over_y(s)

    def begin_late(self, pair, shards):
        first, second = shards[pair[0]], shards[pair[1]]
        blocks = jnp.stack([first, self.over_x(first), second, self.over_y(second)])
        return pair, blocks

    def gather_late(self, state, after):
        pair, blocks = state
        return pair, lax.all_gather(tie(blocks, after), "dp", axis=0, axis_index_groups=self.z_groups)

    def complete_late(self, state, after):
        pair, held = state
        cut = tie(held, after)
        return pair, held, self.over_y(cut[:, :2]), self.over_x(cut[:, 2:])

    def swap_late(self, state, after):
        pair, mine = state[0], state[1:]
        other = [self.over_core(mine[0])] + [self.over_core(k) for k in tie(mine[1:], after)]
        out = {pair[0]: [], pair[1]: []}
        for x in range(2):
            for k in (mine, other):
                out[pair[0]].append([(k[0], x), (k[1], x)])
                out[pair[1]].append([(k[2 * x], 2 - 2 * x), (k[2 * x], 3 - 2 * x)])
        return out

    def begun(self, state):
        return state[3:]

    def complete(self, state, after):
        pair, s, u, t = state
        cut_t, cut_u = tie((t, u), after)
        v0, v1 = self.over_x(cut_t[:, 0:1]), self.over_y(cut_u[:, 1:2])
        mine = (s, t, u, v0, v1)
        other = [self.over_core(k) for k in mine]
        out = {}
        for m, name in enumerate(pair):
            out[name] = [
                [(k[0], m), (k[1], m)] if j < 2 else [(k[2], m), (k[3 + m], 0)] for j, k in enumerate((mine, other, mine, other))
            ]
        return out

    def swap_out(self, stash):
        keep, send = stash
        return [keep, self.over_core(send)]

    def fold(self, items, after=()):
        stashes, kinds = weight_kinds(items)
        n, cols = len(items), stashes[0].shape[2]
        half = cols // 2
        cut = cols if n == 2 else cols // 2
        outs = (shape((n, half, cols), BF16),) * 3 + (shape((half, cut), BF16),) * 2
        s, t, u, va, vb = small(functools.partial(grad_kernel, kinds, 2), stashes, outs, 3, 30, after)
        return s, t, u, va, vb

    def send(self, state, after=()):
        s, t, u, va, vb = state
        va, vb = tie((va, vb), after)
        return s, t, u, self.over_x(va), self.over_y(vb)

    def bump_spec(self, state, after=()):
        s, t, u, ra, rb = state
        t, u = tie((t, u), after)
        return bump_kernel, [t, u, ra, rb], [shape(t.shape, BF16), shape(u.shape, BF16)]

    def bump(self, *states, after=()):
        done = several([self.bump_spec(k, after) for k in states], 1.5 * len(states))
        return [(k[0], t, u) for k, (t, u) in zip(states, done)]

    def merge_spec(self, state, after=()):
        s, rt, ru, _ = state
        n, half, cols = s.shape
        return close_kernel, [tie(s, after), rt, ru], [shape((4, n, half // 4, cols), BF16)]

    def merge_and_bump(self, state, *others, after=()):
        done = several([self.merge_spec(state, after)] + [self.bump_spec(k, after) for k in others], 1.5 + 1.5 * len(others))
        return [done[0][0]] + [(k[0], t, u) for k, (t, u) in zip(others, done[1:])]

    def go(self, state, after=()):
        s, t, u = state
        cut_t, cut_u = tie((t, u), after)
        return s, self.over_y(cut_t), self.over_x(cut_u), t

    def landed(self, state):
        return state[1:3]

    def merge(self, state, after=()):
        return several([self.merge_spec(state, after)], 1.5)[0][0]

    def close(self, both):
        n = both.shape[1]
        if n == 1:
            return [self.z_scatter(both)[0]]
        both = lax.psum_scatter(both, "dp", scatter_dimension=0, axis_index_groups=self.z_groups)
        return [both[i] for i in range(n)]

    def gate(self, state):
        if not isinstance(state, tuple):
            return [state]
        return [state[{3: 1, 4: 3, 5: 0}[len(state)]]]

    def first_totals(self, value):
        for axis, mask in (("tensor", 1), ("dp", 2), ("dp", 4)):
            value = value + self.swap(value, axis, mask)
        return value

    def next_total(self, value, axis, after):
        other = self.over_x(value) if axis == "x" else self.over_y(value)
        return value + tie(other, after)


def adam_step(weight, gradient, first, second, rate):
    first_new = decay_one * first + (1.0 - decay_one) * gradient
    second_new = decay_two * second + (1.0 - decay_two) * gradient * gradient
    fix_one = 1.0 - decay_one**STEP
    fix_two = 1.0 - decay_two**STEP
    ratio = first_new / fix_one / (jnp.sqrt(second_new / fix_two) + adam_eps)
    return (first_new, second_new, weight - rate * (ratio + weight_decay * weight))


def mm(left, right):
    return jnp.dot(left, right, preferred_element_type=F32)


def mm_nt(left, right):
    return lax.dot_general(left, right, (((1,), (1,)), ((), ())), preferred_element_type=F32)


def mm_tn(left, right):
    return lax.dot_general(left, right, (((0,), (0,)), ((), ())), preferred_element_type=F32)


def normed(z, gain, shift):
    centered = z - jnp.mean(z, axis=-1, keepdims=True)
    scale = lax.rsqrt(jnp.mean(centered * centered, axis=-1, keepdims=True) + lnorm_eps)
    xhat = centered * scale
    return xhat * gain + shift, xhat, scale


def norm_back(g, xhat, scale, gain, sums_ref):
    gg = g * gain
    g_z = (gg - jnp.mean(gg, axis=-1, keepdims=True) - xhat * jnp.mean(gg * xhat, axis=-1, keepdims=True)) * scale
    sums_ref[...] = jnp.zeros(sums_ref.shape, F32)
    sums_ref[0:1, :] = jnp.sum(g_z, axis=0, keepdims=True)
    sums_ref[1:2, :] = jnp.sum(g * xhat, axis=0, keepdims=True)
    sums_ref[2:3, :] = jnp.sum(g, axis=0, keepdims=True)
    return g_z


def put_adam(refs, at, gradient, rate):
    w_ref, m_ref, v_ref, g_out, m_out, v_out, w_out, copy_out = refs
    m_new, v_new, w_new = adam_step(w_ref[at], gradient, m_ref[at], v_ref[at], rate)
    g_out[at], m_out[at], v_out[at], w_out[at] = gradient, m_new, v_new, w_new
    copy_out[at] = w_new.astype(BF16)


def adam_ffn_kernel(ins, outs, up_ref, down_ref):
    put_adam(ins[:3] + outs[:5], 0, up_ref[...].astype(F32), rate_up)
    put_adam(ins[3:] + outs[5:], 0, down_ref[...].astype(F32), rate_down)


def adam_att_kernel(ins, outs, share_ref):
    g = share_ref[...].astype(F32)
    cols = ins[0].shape[3]
    for i in range(3):
        put_adam(ins[:3] + outs[:5], (0, i), g[:, i * cols : (i + 1) * cols], rate_in)
    put_adam(ins[3:] + outs[5:], 0, g[:, 3 * cols :].T, rate_out)


def adam_call(kernel, at, shares, groups, earlier):
    flat_in = [a for g in groups for a in g]

    def one(a):
        return pl.BlockSpec((1,) + a.shape[1:], lambda i: at + (0,) * (len(a.shape) - 1))

    outs = []
    for g in groups:
        outs += [shape(g[0].shape)] * 4 + [shape(g[0].shape, BF16)]
    n, n_in, old = len(shares), len(flat_in), list(earlier or ())

    def body(*refs):
        kernel(refs[n : n + n_in], refs[n + n_in + len(old) :], *refs[:n])

    return pl.pallas_call(
        body,
        grid=(1,),
        in_specs=[pl.BlockSpec(a.shape, lambda i: (0, 0)) for a in shares] + [one(a) for a in flat_in] + [pl.BlockSpec(memory_space=pl.ANY)] * len(old),
        out_specs=tuple(one(o) for o in outs),
        out_shape=tuple(outs),
        input_output_aliases={n + n_in + i: i for i in range(len(old))},
        cost_estimate=work(3),
        compiler_params=pltpu.CompilerParams(vmem_limit_bytes=24 * MIB),
    )(*shares, *flat_in, *old)


def head_lanes(hn, width):
    lane = lax.broadcasted_iota(jnp.int32, (1, width), 1) // HD
    return [lane == h for h in range(hn)]


def stacked(value, lanes):
    return jnp.concatenate([jnp.where(m, value, 0.0) for m in lanes], axis=0).astype(BF16)


def gathered(value, lanes):
    rows = value.shape[0] // len(lanes)
    parts = [jnp.where(m, value[h * rows : (h + 1) * rows], 0.0) for h, m in enumerate(lanes)]
    return sum(parts[1:], parts[0])


def probabilities(q_rows, k, mask):
    rows = mask.shape[0]
    s = mm_nt(q_rows, k).reshape(-1, rows, rows) * HD ** (-0.5)
    s = jnp.where(mask[None] > 0, s, -1e30)
    e = jnp.exp(s - jnp.max(s, axis=-1, keepdims=True))
    return (e / jnp.sum(e, axis=-1, keepdims=True)).reshape(-1, rows)


def att_fwd_kernel(n, nw, hn, x_ref, mask_ref, bias_ref, vec_ref, *refs):
    w, (out_ref, xhat_ref, scale_ref, qkv_ref, mix_ref) = split(refs[:nw], n), refs[nw:]
    c, lanes = hn * HD, head_lanes(hn, 256)
    x = x_ref[...]
    x16 = x.astype(BF16)
    z = x + vec_ref[0:1, :]
    for j in range(n):
        blank = jnp.zeros((1, c), F32)
        bias = jnp.concatenate([bias_ref[0:1, j * c : (j + 1) * c], blank, bias_ref[1:2, j * c : (j + 1) * c], blank], axis=1)
        qkv = times(x16, w[j]) + bias
        k = pltpu.roll(qkv[:, c - 64 : c + 192], 192, 1).astype(BF16)
        q, v = qkv[:, :256].astype(BF16), qkv[:, 2 * c : 2 * c + 256].astype(BF16)
        qkv_ref[j, :, :256], qkv_ref[j, :, 256:512], qkv_ref[j, :, 512:] = q, k, v
        p = probabilities(stacked(q.astype(F32), lanes), k, mask_ref[...]).astype(BF16)
        mix = pltpu.roll(gathered(mm(p, v), lanes), 64, 1).astype(BF16)
        mix_ref[j] = mix
        z = z + times_t(mix, w[j], 3 * c - 64)
    out, xhat, scale = normed(z, vec_ref[1:2, :], vec_ref[2:3, :])
    out_ref[...] = out
    xhat_ref[...] = xhat
    scale_ref[...] = jnp.broadcast_to(scale, scale_ref.shape)


def att_bwd_kernel(n, nw, hn, g_ref, x_ref, mask_ref, vec_ref, xhat_ref, scale_ref, qkv_ref, mix_ref, *refs):
    w, (gin_ref, sums_ref, bias_ref), stash = split(refs[:nw], n), refs[nw : nw + 3], refs[nw + 3 :]
    c, lanes, groups = hn * HD, head_lanes(hn, 256), len(stash)
    g_z = norm_back(g_ref[...], xhat_ref[...], scale_ref[:, 0:1], vec_ref[1:2, :], sums_ref)
    wide, x16 = g_z.astype(BF16), x_ref[...].astype(BF16)
    for ref in stash:
        ref[0], ref[1] = x16, wide
    gin = g_z
    for j in range(n):
        q, k, v = qkv_ref[j, :, :256], qkv_ref[j, :, 256:512], qkv_ref[j, :, 512:]
        d_mix = pltpu.roll(times_from(wide, w[j], 3 * c - 64), 192, 1).astype(BF16)
        da, q = stacked(d_mix.astype(F32), lanes), stacked(q.astype(F32), lanes)
        p = probabilities(q, k, mask_ref[...])
        dv = mm_tn(p.astype(BF16), da)
        dp = mm_nt(da, v)
        ds = (p * (dp - jnp.sum(p * dp, axis=-1, keepdims=True))).astype(BF16) * HD ** (-0.5)
        dq = gathered(mm(ds, k), lanes)
        dk = pltpu.roll(mm_tn(ds, q), 64, 1)
        front = [dq[:, :128], dq[:, 128:] + dk[:, :128], dk[:, 128:], dv[:, :128]]
        d_qkv = jnp.concatenate(front + [dv[:, 128:]], axis=1).astype(BF16)
        sums = jnp.sum(d_qkv.astype(F32), axis=0, keepdims=True)
        bias_ref[0:1, j * c : (j + 1) * c] = sums[:, :c]
        bias_ref[1:2, j * c : (j + 1) * c] = sums[:, 2 * c : 3 * c]
        place = stash[j % groups].at[2 + j // groups]
        place[:, :512] = d_qkv[:, :512]
        place[:, 512:640] = d_qkv[:, 512:] + mix_ref[j, :, :128]
        place[:, 640:] = mix_ref[j, :, 128:]
        gin = gin + times_t(d_qkv, w[j], 0, 640)
    gin_ref[...] = gin


def ffn_kernel(n, nw, x_ref, cot_ref, bias_ref, vec_ref, *refs):
    up, down = split(refs[:nw], n), split(refs[nw : 2 * nw], n)
    out_ref, gin_ref, sums_ref, dbias_ref = refs[2 * nw : 2 * nw + 4]
    slope_ref, stash = refs[-1], refs[2 * nw + 4 : -1]
    groups, held = len(stash), n // len(stash)
    x = x_ref[...]
    x16 = x.astype(BF16)
    z = x + vec_ref[0:1, :]
    for j in range(n):
        inner = times(x16, up[j]) + bias_ref[j : j + 1, :]
        half = 0.5 * (1.0 + lax.erf(inner * 0.7071067811865476))
        act = (inner * half).astype(BF16)
        slope_ref[j] = half + inner * (0.3989422804014327 * jnp.exp(-0.5 * inner * inner))
        stash[j % groups][2 + j // groups] = act
        z = z + times_t(act, down[j])
    out, xhat, scale = normed(z, vec_ref[1:2, :], vec_ref[2:3, :])
    out_ref[...] = out
    g_z = norm_back(cot_ref[...].astype(F32), xhat, scale, vec_ref[1:2, :], sums_ref)
    wide = g_z.astype(BF16)
    for ref in stash:
        ref[0], ref[1] = x16, wide
    gin = g_z
    for j in range(n):
        d_inner = (times(wide, down[j]) * slope_ref[j]).astype(BF16)
        dbias_ref[j : j + 1, :] = jnp.sum(d_inner.astype(F32), axis=0, keepdims=True)
        stash[j % groups][2 + held + j // groups] = d_inner
        gin = gin + times_t(d_inner, up[j])
    gin_ref[...] = gin


def weight_grad(kind, refs, i, held):
    total = None
    for ref in refs:
        if kind == "d":
            part = mm_tn(ref[1], ref[2 + i])
        elif kind == "u":
            part = mm_tn(ref[0], ref[2 + held + i])
        else:
            both = ref[2 + i]
            part = mm_tn(ref[0], both)
            tail = mm_tn(ref[1], both[:, 512:])
            own = lax.broadcasted_iota(jnp.int32, (1, 256), 1) < 64
            part = jnp.concatenate([part[:, :512], jnp.where(own, part[:, 512:], tail)], axis=1)
        total = part if total is None else total + part
    return total.astype(BF16)


def grad_kernel(kinds, held, *refs):
    outs = refs[-5:]
    s_ref, t_ref, u_ref, va_ref, vb_ref = outs
    for m, (kind, at) in enumerate(kinds):
        g = weight_grad(kind, [refs[i] for i in at], 1, held)
        half = g.shape[0] // 2
        u_ref[m], v = g[:half], g[half:]
        if len(kinds) == 1:
            va_ref[...], vb_ref[...] = v[:, : v.shape[1] // 2], v[:, v.shape[1] // 2 :]
        elif m == 0:
            va_ref[...] = v
        else:
            vb_ref[...] = v
        g = weight_grad(kind, [refs[i] for i in at], 0, held)
        s_ref[m], t_ref[m] = g[:half], g[half:]


def grad_plain_kernel(kinds, held, *refs):
    for m, (kind, at) in enumerate(kinds):
        for i in range(held):
            refs[len(refs) - len(kinds) + m][i] = weight_grad(kind, [refs[k] for k in at], i, held)


def bump_kernel(t_ref, u_ref, a_ref, b_ref, t_out, u_out):
    cut, cols, last = a_ref.shape[1], t_ref.shape[2], u_ref.shape[0] - 1
    t_out[...] = t_ref[...]
    u_out[...] = u_ref[...]
    t_out[0, :, :cut] = (t_ref[0, :, :cut].astype(F32) + a_ref[...].astype(F32)).astype(BF16)
    u_out[last, :, cols - cut :] = (u_ref[last, :, cols - cut :].astype(F32) + b_ref[...].astype(F32)).astype(BF16)


def close_kernel(s_ref, t_ref, u_ref, out_ref):
    n, rows = s_ref.shape[0], s_ref.shape[1] // 4
    for m in range(n):
        for z in range(4):
            at = slice(z * rows, (z + 1) * rows)
            out_ref[z, m] = (s_ref[m, at].astype(F32) + t_ref[m, at].astype(F32) + u_ref[m, at].astype(F32)).astype(BF16)


def small(kernel, args, outs, micros, limit=24, after=()):
    vmem, n_in = pl.BlockSpec(memory_space=pltpu.VMEM), len(args)

    def body(*refs):
        kernel(*refs[:n_in], *refs[n_in + len(after) :])

    return pl.pallas_call(
        body,
        in_specs=[vmem] * n_in + [pl.BlockSpec(memory_space=pl.ANY)] * len(after),
        out_specs=tuple([vmem] * len(outs)),
        out_shape=tuple(outs),
        cost_estimate=work(micros),
        compiler_params=pltpu.CompilerParams(vmem_limit_bytes=limit * MIB),
    )(*args, *after)


def several(specs, micros):
    def body(*refs):
        at, out = 0, sum(len(s[1]) for s in specs)
        for kernel, args, outs in specs:
            kernel(*refs[at : at + len(args)], *refs[out : out + len(outs)])
            at, out = at + len(args), out + len(outs)

    res = list(small(body, [a for s in specs for a in s[1]], [o for s in specs for o in s[2]], micros, 40))
    return [[res.pop(0) for _ in s[2]] for s in specs]


def flat(ref):
    k, _, r, c = ref.shape
    return ref[...].reshape(k * r, c)


def times(x, refs):
    total, at = None, 0
    for ref in refs:
        w = flat(ref)
        part = mm(x[:, at : at + w.shape[0]], w)
        total = part if total is None else total + part
        at += w.shape[0]
    return total


def times_t(x, refs, start=0, stop=None):
    return jnp.concatenate([mm_nt(x, flat(ref)[:, start:stop]) for ref in refs], axis=1)


def times_from(x, refs, start):
    total, at = None, 0
    for ref in refs:
        w = flat(ref)[:, start:]
        part = mm(x[:, at : at + w.shape[0]], w)
        total = part if total is None else total + part
        at += w.shape[0]
    return total


def split(refs, n):
    size = len(refs) // n
    return [refs[i * size : (i + 1) * size] for i in range(n)]


MIB = 1024 * 1024
SCALE = 0.2


def work(micros):
    return pl.CostEstimate(flops=int(micros * SCALE * 1.1e9), bytes_accessed=1024, transcendentals=0)


def call(kernel, args, weights, outs, cost, vmem, after=(), scratch=()):
    chunks = [c for piece in weights for c in piece]
    n_in, waits = len(args) + len(chunks), len(after)

    def body(*refs):
        kernel(*refs[:n_in], *refs[n_in + waits :])

    once = pl.Buffered(buffer_count=1)

    def whole(a):
        return pl.BlockSpec(a.shape, lambda i, nd=len(a.shape): (0,) * nd, pipeline_mode=once)

    def picked(a, m):
        k, _, r, c = a.shape
        return pl.BlockSpec((k, 1, r, c), lambda i: (0, m, 0, 0), pipeline_mode=once)

    return pl.pallas_call(
        body,
        grid=(1,),
        out_shape=tuple(outs),
        scratch_shapes=list(scratch),
        in_specs=[whole(a) for a in args] + [picked(a, m) for a, m in chunks]
        + [pl.BlockSpec(memory_space=pl.ANY)] * waits,
        out_specs=tuple(whole(o) for o in outs),
        compiler_params=pltpu.CompilerParams(vmem_limit_bytes=vmem * MIB),
        cost_estimate=cost,
    )(*args, *[a for a, m in chunks], *after)


def shape(dims, kind=F32):
    return jax.ShapeDtypeStruct(dims, kind)


def dims_of(piece):
    return [a.shape[0] * a.shape[2] for a, m in piece], piece[0][0].shape[3]


def count(w):
    return len(w), sum(len(p) for p in w)


def att_forward(x, mask, bias, vec, w, hn):
    (n, nw), (rows, width) = count(w), x.shape
    outs = [shape((rows, width)), shape((rows, width)), shape((rows, 128)), shape((n, rows, 768), BF16), shape((n, rows, 256), BF16)]
    return call(functools.partial(att_fwd_kernel, n, nw, hn), [x, mask, bias, vec], w, outs, work(4 + rows / 50), 30)


def att_backward(g, x, mask, vec, kept, w, hn, groups, after=()):
    (n, nw), (rows, width) = count(w), x.shape
    outs = [shape((rows, width)), shape((8, width)), shape((2, width))] + [shape((2 + n // groups, rows, width), BF16)] * groups
    res = call(functools.partial(att_bwd_kernel, n, nw, hn), [g, x, mask, vec] + list(kept), w, outs, work(4 + rows / 26), 30, after)
    return res[0], res[1], res[2], res[3:]


def ffn_both(x, cot, bias, vec, up, down, groups, after=()):
    (n, nw), (rows, width), f = count(up), x.shape, dims_of(up[0])[1]
    outs = [shape((rows, width)), shape((rows, width)), shape((8, width)), shape((n, f))]
    outs += [shape((2 + 2 * n // groups, rows, width), BF16)] * groups
    scratch = [pltpu.VMEM((n, rows, f), F32)]
    res = call(functools.partial(ffn_kernel, n, nw), [x, cot, bias, vec], up + down, outs, work(7 + rows / 50), 38, after, scratch)
    return res[0], res[1], res[2], res[3], res[4:]


def weight_kinds(items):
    stashes = []
    kinds = []
    for kind, arrays in items:
        at = []
        for array in arrays:
            same = [i for i, s in enumerate(stashes) if s is array]
            at.append(same[0] if same else len(stashes))
            stashes += [] if same else [array]
        kinds.append((kind, tuple(at)))
    return stashes, tuple(kinds)


def make_local(mesh):
    n_t = mesh.shape["tensor"]
    net = (Grid if (mesh.shape["dp"], n_t) == (8, 4) else Plain)(mesh)

    def local(
        lang_in, visn_in, word_len, lang_cot, visn_cot, att_in, att_out, ffn_up, ffn_down, vectors, ffn_bias1,
        att_in_m, att_in_v, att_out_m, att_out_v, ffn_up_m, ffn_up_v, ffn_down_m, ffn_down_v,
        vectors_m, vectors_v, bias1_m, bias1_v,
    ):
        width = lang_in.shape[1]
        rows = att_in.shape[1]
        cols = att_in.shape[3]
        ff = ffn_up.shape[2]
        heads_here = cols // HD
        items = word_len.shape[0]
        usable = jnp.arange(LW, dtype=jnp.int32)[None, :] < word_len[:, None]

        shards = {}
        for b in range(3):
            shards["a%d" % b] = jnp.concatenate(
                [att_in[b].astype(BF16).reshape(rows, 3 * cols), att_out[b].astype(BF16).T], axis=1
            )
        for i in range(2):
            shards["u%d" % i] = ffn_up[i].astype(BF16)
            shards["d%d" % i] = ffn_down[i].astype(BF16).T

        index_of = (net.row_blocks()[:, None] * rows + jnp.arange(rows, dtype=jnp.int32)[None, :]).reshape(-1)
        turn = (jnp.arange(width, dtype=jnp.int32)[:, None] == index_of[None, :])
        turn16, turn32 = turn.astype(BF16), turn.astype(F32)

        def to_rel(value):
            return mm(value, turn16).astype(BF16)

        def to_abs(value):
            return lax.dot_general(value, turn32, (((1,), (1,)), ((), ())), precision=HIGHEST)

        pieces = jnp.stack([net.piece_at(j) for j in range(n_t)])
        chosen = pieces[:, None] == jnp.arange(n_t, dtype=jnp.int32)[None, :]
        column = (pieces[:, None] * cols + jnp.arange(cols, dtype=jnp.int32)[None, :]).reshape(-1)
        turn_heads = (jnp.arange(width, dtype=jnp.int32)[:, None] == column[None, :]).astype(F32)

        def by_piece(value):
            return jnp.sum(jnp.where(chosen[None, :, :, None], value[:, None], 0.0), axis=2)

        vec = jnp.dot(vectors, turn32, precision=HIGHEST)
        vec_heads = jnp.dot(vectors, turn_heads, precision=HIGHEST)
        bias_ff = by_piece(ffn_bias1.reshape(2, n_t, ff))
        qv = [vec_heads[5 * b : 5 * b + 2] for b in range(3)]

        def rows3(row):
            return vec[row : row + 3]

        n_lang, n_visn = lang_in.shape[0], visn_in.shape[0]
        slots, regions = n_lang // items, n_visn // items
        item = jnp.concatenate([jnp.arange(n_lang) // slots, jnp.arange(n_visn) // regions])
        is_lang = jnp.arange(n_lang + n_visn) < n_lang
        seen = jnp.concatenate([usable.reshape(-1), jnp.ones((n_visn,), bool)])
        same = (item[:, None] == item[None, :]) & seen[None, :]
        mask0 = (same & (is_lang[:, None] != is_lang[None, :])).astype(F32)
        mask1 = same[:n_lang, :n_lang].astype(F32)
        mask2 = same[n_lang:, n_lang:].astype(F32)

        x0 = to_rel(jnp.concatenate([lang_in, visn_in], axis=0)).astype(F32)
        full = net.first(shards)
        later = tie({k: v for k, v in shards.items() if k != "a0"}, shards["a0"])
        pair1 = net.begin(("a1", "a2"), later, ())
        pair3 = net.begin_late(("u1", "d1"), later)
        both1, *kept0 = att_forward(x0, mask0, qv[0], rows3(2), full["a0"], heads_here)
        pair3 = net.gather_late(pair3, both1)
        full.update(net.complete(pair1, both1))
        pair2 = net.begin(("u0", "d0"), later, net.begun(pair1))
        lang1, visn1 = both1[:n_lang], both1[n_lang:]
        lang2, *kept1 = att_forward(lang1, mask1, qv[1], rows3(7), full["a1"], heads_here)
        visn2, *kept2 = att_forward(visn1, mask2, qv[2], rows3(12), full["a2"], heads_here)
        full.update(net.complete(pair2, (lang2, visn2)))
        pair3 = net.complete_late(pair3, full["d0"][-1][-1][0])
        groups = net.groups
        lang_out, g_lang, sums15, bias_lang, stash = ffn_both(lang2, to_rel(lang_cot), bias_ff[0], rows3(15), full["u0"], full["d0"], groups)
        rows_f0 = net.swap_out(stash)
        g_lang, sums7, bias1, stash = att_backward(g_lang, lang1, mask1, rows3(7), kept1, full["a1"], heads_here, groups)
        rows_a1 = net.swap_out(stash)
        part0 = net.send(net.fold([("d", rows_f0), ("u", rows_f0)], [sums7]))
        full.update(net.swap_late(pair3, net.gate(part0)))
        first = ffn_both(visn2, to_rel(visn_cot), bias_ff[1], rows3(18), full["u1"], full["d1"], groups, net.gate(part0))
        (part0,) = net.bump(part0, after=first[2])
        visn_out, g_visn, sums18, bias_visn, stash = tie(first, net.gate(part0))
        part0 = net.go(part0)
        rows_f1 = net.swap_out(stash)
        part1 = net.fold([("d", rows_f1), ("u", rows_f1)], net.gate(part0))
        first = att_backward(g_visn, visn1, mask2, rows3(12), kept2, full["a2"], heads_here, groups, net.gate(part0) + net.gate(part1))
        g_visn, sums12, bias2, stash = tie(first, net.landed(part0))
        part1 = net.send(part1, net.landed(part0))
        rows_a2 = net.swap_out(stash)
        part2 = net.send(net.fold([("a", rows_a1), ("a", rows_a2)], net.gate(part1)))
        first = att_backward(
            jnp.concatenate([g_lang, g_visn], axis=0), x0, mask0, rows3(2), kept0, full["a0"], heads_here, groups, net.gate(part2)
        )
        part0, part1, part2 = net.merge_and_bump(part0, part1, part2, after=first[1])
        share0 = net.close(part0)
        g_both, sums2, bias0, stash = tie(first, net.gate(part1) + net.gate(part2))
        part1 = net.go(part1)
        rows_a0 = net.swap_out(stash)
        part3 = net.send(net.fold([("a", rows_a0)], net.gate(part2)))
        blank = jnp.zeros((2, width), F32)
        by_rows = to_abs(jnp.concatenate([blank, sums2[:3], blank, sums7[:3], blank, sums12[:3], sums15[:3], sums18[:3]], axis=0))
        by_heads = lax.dot_general(
            jnp.concatenate([bias0, bias1, bias2], axis=0), turn_heads, (((1,), (1,)), ((), ())), precision=HIGHEST
        )
        out_abs = to_abs(jnp.concatenate([lang_out, visn_out, g_both], axis=0))
        n_both = n_lang + n_visn
        lang_out, visn_out = out_abs[:n_lang], out_abs[n_lang:n_both]
        lang_grad, visn_grad = out_abs[n_both : n_both + n_lang], out_abs[n_both + n_lang :]

        whole = []
        for b in range(3):
            whole += [by_heads[2 * b : 2 * b + 2], by_rows[5 * b + 2 : 5 * b + 5]]
        by_rows = jnp.concatenate(whole + [by_rows[15:]], axis=0)
        bias_all = by_piece(jnp.stack([bias_lang, bias_visn]))
        sums = net.first_totals(tie(jnp.concatenate([by_rows, bias_all.reshape(-1, width)], axis=0), net.gate(part3)))
        part2 = net.go(part2, net.landed(part1))
        part1, part3 = net.merge_and_bump(part1, part3, after=sums)
        part3 = net.go(part3)
        share1 = net.close(part1)
        part2 = net.merge(part2, net.gate(part1))
        share2 = net.close(part2)

        t_in, t_in_m, t_in_v = (jnp.transpose(k, (0, 2, 1, 3)) for k in (att_in, att_in_m, att_in_v))
        up_all = (ffn_up, ffn_up_m, ffn_up_v)
        down_all = [jnp.transpose(k, (0, 2, 1)) for k in (ffn_down, ffn_down_m, ffn_down_v)]
        ffn_new = adam_call(adam_ffn_kernel, (0,), share0[1::-1], [up_all, down_all], None)
        ffn_new = adam_call(adam_ffn_kernel, (1,), share1[1::-1], [up_all, down_all], ffn_new)
        sums = net.next_total(sums, "x", net.gate(part3))
        part3 = net.merge(part3, ffn_new[0])
        sums = net.next_total(sums, "y", net.gate(part3))
        share3 = net.close(part3)
        vector_grad, bias1_grad = sums[:21], sums[21:].reshape(ffn_bias1.shape)

        att_all = [(t_in, t_in_m, t_in_v), (att_out, att_out_m, att_out_v)]
        att_new = adam_call(adam_att_kernel, (1,), share2[:1], att_all, None)
        att_new = adam_call(adam_att_kernel, (2,), share2[1:], att_all, att_new)
        att_new = adam_call(adam_att_kernel, (0,), share3, att_all, att_new)
        in_new = [jnp.transpose(k, (0, 2, 1, 3)) for k in att_new[:5]]

        result = [lang_out, visn_out, lang_grad, visn_grad] + in_new + list(att_new[5:]) + list(ffn_new[:5]) + [jnp.transpose(k, (0, 2, 1)) for k in ffn_new[5:]]
        for share, weight, first, second, rate in (
            (vector_grad, vectors, vectors_m, vectors_v, rate_vector),
            (bias1_grad, ffn_bias1, bias1_m, bias1_v, rate_bias),
        ):
            m_new, v_new, w_new = adam_step(weight, share, first, second, rate)
            result += [share, m_new, v_new, w_new]
        return tuple(result)

    return local


def solution(mesh):
    rows = P(("dp", "tensor"), None)
    w_in, w_out, w_up, w_down = P(None, "dp", None, "tensor"), P(None, "tensor", "dp"), P(None, "dp", "tensor"), P(None, "tensor", "dp")
    return jax.shard_map(
        make_local(mesh),
        mesh=mesh,
        in_specs=(rows, rows, P(("dp", "tensor")), rows, rows, w_in, w_out, w_up, w_down, P(), P())
        + (w_in,) * 2 + (w_out,) * 2 + (w_up,) * 2 + (w_down,) * 2 + (P(),) * 4,
        out_specs=(rows,) * 4 + (w_in,) * 5 + (w_out,) * 5 + (w_up,) * 5 + (w_down,) * 5 + (P(),) * 8,
        check_vma=False,
    )
```

```python
import functools

import jax
import jax.numpy as jnp
from jax import lax
from jax.experimental import pallas as pl
from jax.experimental.pallas import tpu as pltpu
from jax.sharding import PartitionSpec as P

HD = 64
LW = 20
STEP = 10

lnorm_eps = 1e-12
decay_one = 0.5
decay_two = 0.5
adam_eps = 1e-08
weight_decay = 0.01
rate_in = 0.03
rate_out = 0.1
rate_up = 0.03
rate_down = 0.015
rate_vector = 0.2
rate_bias = 0.2

F32 = jnp.float32
BF16 = jnp.bfloat16
HIGHEST = lax.Precision.HIGHEST

def tie(value, after):
    return lax.optimization_barrier((value, after))[0]


def listed(*values):
    return jax.tree.leaves(values)


class Plain:
    def __init__(self, mesh):
        self.n_dp, self.n_t = mesh.shape["dp"], mesh.shape["tensor"]
        self.groups = 1

    def row_blocks(self):
        return jnp.arange(self.n_dp, dtype=jnp.int32)

    def piece_at(self, j):
        return jnp.int32(j)

    def gather(self, shard):
        whole = lax.all_gather(shard, "dp", axis=0)[:, None]
        for_all = lax.all_gather(whole, "tensor", axis=0)
        return [[(for_all[j], 0)] for j in range(self.n_t)]

    def first(self, shards):
        return (), {"a0": self.gather(shards["a0"])}

    def begin(self, pair, shards, after):
        return {name: self.gather(shards[name]) for name in pair}

    def begin_late(self, pair, shards):
        return self.begin(pair, shards, ())

    def gather_late(self, state, after):
        return state

    def complete_late(self, state, after):
        return state

    def swap_late(self, state, after):
        return state

    def begun(self, state):
        return ()

    def complete(self, state, after):
        return state

    def swap_out(self, stash):
        return list(stash)

    def fold(self, items, after=()):
        stashes, kinds = weight_kinds(items)
        outs = [shape((self.n_t, stashes[0].shape[2], stashes[0].shape[2]), BF16)] * len(items)
        return small(functools.partial(grad_plain_kernel, kinds, self.n_t), stashes, outs, 8, 40, after)

    def fold_wide(self, items, after=()):
        return self.fold(items, after)

    def send(self, state, after=()):
        return state

    def bump(self, *states, after=()):
        return list(states)

    def merge_and_bump(self, state, *others, after=()):
        return [state, *others]

    def go(self, state, after=()):
        return state

    def landed(self, state):
        return ()

    def merge(self, state, after=()):
        return state

    def rest(self, shares):
        return shares

    def over_z(self, state, after=()):
        out = []
        for full in state:
            mine = lax.psum_scatter(full, "tensor", scatter_dimension=0)
            out.append(lax.psum_scatter(mine, "dp", scatter_dimension=0, tiled=True))
        return out

    def gate(self, state):
        return []

    def first_totals(self, value):
        return lax.psum(value, ("dp", "tensor"))

    def next_total(self, value, axis, after):
        return value


class Grid:
    def __init__(self, mesh):
        self.n_dp, self.n_t = mesh.shape["dp"], mesh.shape["tensor"]
        self.groups = 2
        self.z_groups = [[z * 2 + y for z in range(4)] for y in range(2)]

    def row_blocks(self):
        y = lax.axis_index("dp") % 2
        return jnp.stack([2 * z + (y ^ k) for k in range(2) for z in range(4)])

    def piece_at(self, j):
        return lax.axis_index("tensor") ^ j

    def swap(self, value, axis, mask):
        size = self.n_dp if axis == "dp" else self.n_t
        return lax.ppermute(value, axis, [(i, i ^ mask) for i in range(size)])

    def over_x(self, value):
        return self.swap(value, "tensor", 2)

    def over_core(self, value):
        return self.swap(value, "tensor", 1)

    def over_y(self, value):
        return self.swap(value, "dp", 1)

    def z_gather(self, value):
        z = lax.axis_index("dp") // 2
        out = jnp.zeros((4,) + value.shape, value.dtype)
        out = lax.dynamic_update_slice_in_dim(out, value[None], z, 0)
        near = self.swap(value, "dp", 2)
        out = lax.dynamic_update_slice_in_dim(out, near[None], z ^ 1, 0)
        for m in range(2, 4):
            out = lax.dynamic_update_slice_in_dim(out, self.swap(value, "dp", 2 * m)[None], z ^ m, 0)
        return out, near

    def z_scatter(self, value, after):
        z = lax.axis_index("dp") // 2
        total = lax.dynamic_index_in_dim(value, z, 0, keepdims=False).astype(F32)
        parts = [lax.dynamic_index_in_dim(value, z ^ m, 0, keepdims=False) for m in range(1, 4)]
        for part in tie([self.swap(part, "dp", 2 * m) for m, part in enumerate(parts, 1)], after):
            total = total + part.astype(F32)
        return total.astype(BF16)

    def first(self, shards):
        s, near = self.z_gather(shards["a0"][None])
        u, t = self.over_x(s), self.over_y(s)
        half = s.shape[-1] // 2
        v = jnp.concatenate([self.over_x(t[..., :half]), self.over_y(u[..., half:])], axis=-1)
        mine = (s, t, u, v)
        other = [self.over_core(k) for k in mine]
        return near, {"a0": [[(k[0], 0), (k[1], 0)] if j < 2 else [(k[2], 0), (k[3], 0)] for j, k in enumerate((mine, other, mine, other))]}

    def begin(self, pair, shards, after):
        s = lax.all_gather(jnp.stack([shards[n] for n in pair]), "dp", axis=0, axis_index_groups=self.z_groups)
        s = tie(s, after)
        return pair, s, self.over_x(s), self.over_y(s)

    def begin_late(self, pair, shards):
        first, second = shards[pair[0]], shards[pair[1]]
        blocks = jnp.stack([first, self.over_x(first), second, self.over_y(second)])
        return pair, blocks

    def gather_late(self, state, after):
        pair, blocks = state
        return pair, lax.all_gather(tie(blocks, after), "dp", axis=0, axis_index_groups=self.z_groups)

    def complete_late(self, state, after):
        pair, held = state
        cut = tie(held, after)
        return pair, held, self.over_y(cut[:, :2]), self.over_x(cut[:, 2:])

    def swap_late(self, state, after):
        pair, mine = state[0], state[1:]
        other = [self.over_core(mine[0])] + [self.over_core(k) for k in tie(mine[1:], after)]
        out = {pair[0]: [], pair[1]: []}
        for x in range(2):
            for k in (mine, other):
                out[pair[0]].append([(k[0], x), (k[1], x)])
                out[pair[1]].append([(k[2 * x], 2 - 2 * x), (k[2 * x], 3 - 2 * x)])
        return out

    def begun(self, state):
        return state[3:]

    def complete(self, state, after):
        pair, s, u, t = state
        cut_t, cut_u = tie((t, u), after)
        v0, v1 = self.over_x(cut_t[:, 0:1]), self.over_y(cut_u[:, 1:2])
        mine = (s, t, u, v0, v1)
        other = [self.over_core(k) for k in mine]
        out = {}
        for m, name in enumerate(pair):
            out[name] = [
                [(k[0], m), (k[1], m)] if j < 2 else [(k[2], m), (k[3 + m], 0)] for j, k in enumerate((mine, other, mine, other))
            ]
        return out

    def swap_out(self, stash):
        keep, send = stash
        return [keep, self.over_core(send)]

    def fold(self, items, after=()):
        stashes, kinds = weight_kinds(items)
        n, cols = len(items), stashes[0].shape[2]
        half = cols // 2
        cut = cols if n == 2 else cols // 2
        outs = (shape((n, half, cols), BF16),) * 3 + (shape((half, cut), BF16),) * 2
        s, t, u, va, vb = small(functools.partial(grad_kernel, kinds, 2), stashes, outs, 3, 30, after)
        return s, t, u, va, vb

    def fold_wide(self, items, after=()):
        stashes, kinds = weight_kinds(items)
        half, cols = stashes[0].shape[2] // 2, stashes[0].shape[2]
        outs = [shape((n, half, cols), BF16) for n in (4, 2, 2)]
        keep, ty, tx = small(functools.partial(grad_wide_kernel, kinds, 2), stashes, outs, 3, 30, after)
        return keep, self.over_y(ty), self.over_x(tx), None

    def send(self, state, after=()):
        s, t, u, va, vb = state
        va, vb = tie((va, vb), after)
        return s, t, u, self.over_x(va), self.over_y(vb)

    def bump_spec(self, state, after=()):
        s, t, u, ra, rb = state
        t, u = tie((t, u), after)
        return bump_kernel, [t, u, ra, rb], [shape(t.shape, BF16), shape(u.shape, BF16)]

    def bump(self, *states, after=()):
        done = several([self.bump_spec(k, after) for k in states], 1.5 * len(states))
        return [(k[0], t, u) for k, (t, u) in zip(states, done)]

    def merge_spec(self, state, after=()):
        s, rt, ru, wide = state
        n, half, cols = s.shape
        if wide is None:
            return close_wide_kernel, [tie(s, after), rt, ru], [shape((4, 4, half // 4, cols), BF16)]
        return close_kernel, [tie(s, after), rt, ru], [shape((4, n, half // 4, cols), BF16)]

    def merge_and_bump(self, state, *others, after=()):
        done = several([self.merge_spec(state, after)] + [self.bump_spec(k, after) for k in others], 1.5 + 1.5 * len(others))
        return [done[0][0]] + [(k[0], t, u) for k, (t, u) in zip(others, done[1:])]

    def go(self, state, after=()):
        s, t, u = state
        cut_t, cut_u = tie((t, u), after)
        return s, self.over_y(cut_t), self.over_x(cut_u), t

    def landed(self, state):
        return state[1:3]

    def merge(self, state, after=()):
        return several([self.merge_spec(state, after)], 1.5)[0][0]

    def over_z(self, both, after=()):
        if both.shape[1] == 1:
            return self.z_scatter(both, after)
        return lax.psum_scatter(both, "dp", scatter_dimension=0, axis_index_groups=self.z_groups)

    def rest(self, held):
        if held.shape[0] == 4:
            return [held[0] + self.over_x(held[1]), held[2] + self.over_y(held[3])]
        return [held[i] for i in range(held.shape[0])]

    def gate(self, state):
        if not isinstance(state, tuple):
            return [state]
        if len(state) == 4:
            return [state[0] if state[3] is None else state[3]]
        return [state[1] if len(state) == 3 else state[0]]

    def first_totals(self, value):
        for axis, mask in (("tensor", 1), ("dp", 2), ("dp", 4)):
            value = value + self.swap(value, axis, mask)
        return value

    def next_total(self, value, axis, after):
        value = tie(value, after)
        return value + (self.over_x(value) if axis == "x" else self.over_y(value))


def adam_step(weight, gradient, first, second, rate):
    first_new = decay_one * first + (1.0 - decay_one) * gradient
    second_new = decay_two * second + (1.0 - decay_two) * gradient * gradient
    fix_one = 1.0 - decay_one**STEP
    fix_two = 1.0 - decay_two**STEP
    ratio = first_new / fix_one / (jnp.sqrt(second_new / fix_two) + adam_eps)
    return (first_new, second_new, weight - rate * (ratio + weight_decay * weight))


def mm(left, right):
    return jnp.dot(left, right, preferred_element_type=F32)


def mm_nt(left, right):
    return lax.dot_general(left, right, (((1,), (1,)), ((), ())), preferred_element_type=F32)


def mm_tn(left, right):
    return lax.dot_general(left, right, (((0,), (0,)), ((), ())), preferred_element_type=F32)


def normed(z, gain, shift):
    centered = z - jnp.mean(z, axis=-1, keepdims=True)
    scale = lax.rsqrt(jnp.mean(centered * centered, axis=-1, keepdims=True) + lnorm_eps)
    xhat = centered * scale
    return xhat * gain + shift, xhat, scale


def norm_back(g, xhat, scale, gain, sums_ref):
    gg = g * gain
    g_z = (gg - jnp.mean(gg, axis=-1, keepdims=True) - xhat * jnp.mean(gg * xhat, axis=-1, keepdims=True)) * scale
    sums_ref[...] = jnp.zeros(sums_ref.shape, F32)
    sums_ref[0:1, :] = jnp.sum(g_z, axis=0, keepdims=True)
    sums_ref[1:2, :] = jnp.sum(g * xhat, axis=0, keepdims=True)
    sums_ref[2:3, :] = jnp.sum(g, axis=0, keepdims=True)
    return g_z


def put_adam(refs, at, gradient, rate):
    w_ref, m_ref, v_ref, g_out, m_out, v_out, w_out, copy_out = refs
    m_new, v_new, w_new = adam_step(w_ref[at], gradient, m_ref[at], v_ref[at], rate)
    g_out[at], m_out[at], v_out[at], w_out[at] = gradient, m_new, v_new, w_new
    copy_out[at] = w_new.astype(BF16)


def adam_ffn_kernel(ins, outs, up_ref, down_ref):
    put_adam(ins[:3] + outs[:5], 0, up_ref[...].astype(F32), rate_up)
    put_adam(ins[3:] + outs[5:], 0, down_ref[...].astype(F32), rate_down)


def adam_att_kernel(ins, outs, share_ref):
    g = share_ref[...].astype(F32)
    cols = ins[0].shape[3]
    for i in range(3):
        put_adam(ins[:3] + outs[:5], (0, i), g[:, i * cols : (i + 1) * cols], rate_in)
    put_adam(ins[3:] + outs[5:], 0, g[:, 3 * cols :].T, rate_out)


def adam_call(kernel, at, shares, groups, earlier):
    flat_in = [a for g in groups for a in g]

    def one(a):
        return pl.BlockSpec((1,) + a.shape[1:], lambda i: at + (0,) * (len(a.shape) - 1))

    outs = []
    for g in groups:
        outs += [shape(g[0].shape)] * 4 + [shape(g[0].shape, BF16)]
    n, n_in, old = len(shares), len(flat_in), list(earlier or ())

    def body(*refs):
        kernel(refs[n : n + n_in], refs[n + n_in + len(old) :], *refs[:n])

    return pl.pallas_call(
        body,
        grid=(1,),
        in_specs=[pl.BlockSpec(a.shape, lambda i: (0, 0)) for a in shares] + [one(a) for a in flat_in] + [pl.BlockSpec(memory_space=pl.ANY)] * len(old),
        out_specs=tuple(one(o) for o in outs),
        out_shape=tuple(outs),
        input_output_aliases={n + n_in + i: i for i in range(len(old))},
        cost_estimate=work(3),
        compiler_params=pltpu.CompilerParams(vmem_limit_bytes=24 * MIB),
    )(*shares, *flat_in, *old)


def head_lanes(hn, width):
    lane = lax.broadcasted_iota(jnp.int32, (1, width), 1) // HD
    return [lane == h for h in range(hn)]


def stacked(value, lanes):
    return jnp.concatenate([jnp.where(m, value, 0.0) for m in lanes], axis=0).astype(BF16)


def gathered(value, lanes):
    rows = value.shape[0] // len(lanes)
    parts = [jnp.where(m, value[h * rows : (h + 1) * rows], 0.0) for h, m in enumerate(lanes)]
    return sum(parts[1:], parts[0])


def probabilities(q_rows, k, mask):
    rows = mask.shape[0]
    s = mm_nt(q_rows, k).reshape(-1, rows, rows) * HD ** (-0.5)
    s = jnp.where(mask[None] > 0, s, -1e30)
    e = jnp.exp(s - jnp.max(s, axis=-1, keepdims=True))
    return (e / jnp.sum(e, axis=-1, keepdims=True)).reshape(-1, rows)


def att_fwd_kernel(n, nw, hn, x_ref, mask_ref, bias_ref, vec_ref, *refs):
    w, (out_ref, xhat_ref, scale_ref, qkv_ref, mix_ref) = split(refs[:nw], n), refs[nw:]
    c, lanes = hn * HD, head_lanes(hn, 256)
    x = x_ref[...]
    x16 = x.astype(BF16)
    z = x + vec_ref[0:1, :]
    for j in range(n):
        blank = jnp.zeros((1, c), F32)
        bias = jnp.concatenate([bias_ref[0:1, j * c : (j + 1) * c], blank, bias_ref[1:2, j * c : (j + 1) * c], blank], axis=1)
        qkv = times(x16, w[j]) + bias
        k = pltpu.roll(qkv[:, c - 64 : c + 192], 192, 1).astype(BF16)
        q, v = qkv[:, :256].astype(BF16), qkv[:, 2 * c : 2 * c + 256].astype(BF16)
        qkv_ref[j, :, :256], qkv_ref[j, :, 256:512], qkv_ref[j, :, 512:] = q, k, v
        p = probabilities(stacked(q.astype(F32), lanes), k, mask_ref[...]).astype(BF16)
        mix = pltpu.roll(gathered(mm(p, v), lanes), 64, 1).astype(BF16)
        mix_ref[j] = mix
        z = z + times_t(mix, w[j], 3 * c - 64)
    out, xhat, scale = normed(z, vec_ref[1:2, :], vec_ref[2:3, :])
    out_ref[...] = out
    xhat_ref[...] = xhat
    scale_ref[...] = jnp.broadcast_to(scale, scale_ref.shape)


def att_bwd_kernel(n, nw, hn, g_ref, x_ref, mask_ref, vec_ref, xhat_ref, scale_ref, qkv_ref, mix_ref, *refs):
    w, (gin_ref, sums_ref, bias_ref), stash = split(refs[:nw], n), refs[nw : nw + 3], refs[nw + 3 :]
    c, lanes, groups = hn * HD, head_lanes(hn, 256), len(stash)
    g_z = norm_back(g_ref[...], xhat_ref[...], scale_ref[:, 0:1], vec_ref[1:2, :], sums_ref)
    wide, x16 = g_z.astype(BF16), x_ref[...].astype(BF16)
    for ref in stash:
        ref[0], ref[1] = x16, wide
    gin = g_z
    for j in range(n):
        q, k, v = qkv_ref[j, :, :256], qkv_ref[j, :, 256:512], qkv_ref[j, :, 512:]
        d_mix = pltpu.roll(times_from(wide, w[j], 3 * c - 64), 192, 1).astype(BF16)
        da, q = stacked(d_mix.astype(F32), lanes), stacked(q.astype(F32), lanes)
        p = probabilities(q, k, mask_ref[...])
        dv = mm_tn(p.astype(BF16), da)
        dp = mm_nt(da, v)
        ds = (p * (dp - jnp.sum(p * dp, axis=-1, keepdims=True))).astype(BF16) * HD ** (-0.5)
        dq = gathered(mm(ds, k), lanes)
        dk = pltpu.roll(mm_tn(ds, q), 64, 1)
        front = [dq[:, :128], dq[:, 128:] + dk[:, :128], dk[:, 128:], dv[:, :128]]
        d_qkv = jnp.concatenate(front + [dv[:, 128:]], axis=1).astype(BF16)
        sums = jnp.sum(d_qkv.astype(F32), axis=0, keepdims=True)
        bias_ref[0:1, j * c : (j + 1) * c] = sums[:, :c]
        bias_ref[1:2, j * c : (j + 1) * c] = sums[:, 2 * c : 3 * c]
        place = stash[j % groups].at[2 + j // groups]
        place[:, :512] = d_qkv[:, :512]
        place[:, 512:640] = d_qkv[:, 512:] + mix_ref[j, :, :128]
        place[:, 640:] = mix_ref[j, :, 128:]
        gin = gin + times_t(d_qkv, w[j], 0, 640)
    gin_ref[...] = gin


def ffn_kernel(n, nw, x_ref, cot_ref, bias_ref, vec_ref, *refs):
    up, down = split(refs[:nw], n), split(refs[nw : 2 * nw], n)
    out_ref, gin_ref, sums_ref, dbias_ref = refs[2 * nw : 2 * nw + 4]
    slope_ref, stash = refs[-1], refs[2 * nw + 4 : -1]
    groups, held = len(stash), n // len(stash)
    x = x_ref[...]
    x16 = x.astype(BF16)
    z = x + vec_ref[0:1, :]
    for j in range(n):
        inner = times(x16, up[j]) + bias_ref[j : j + 1, :]
        half = 0.5 * (1.0 + lax.erf(inner * 0.7071067811865476))
        act = (inner * half).astype(BF16)
        slope_ref[j] = half + inner * (0.3989422804014327 * jnp.exp(-0.5 * inner * inner))
        stash[j % groups][2 + j // groups] = act
        z = z + times_t(act, down[j])
    out, xhat, scale = normed(z, vec_ref[1:2, :], vec_ref[2:3, :])
    out_ref[...] = out
    g_z = norm_back(cot_ref[...].astype(F32), xhat, scale, vec_ref[1:2, :], sums_ref)
    wide = g_z.astype(BF16)
    for ref in stash:
        ref[0], ref[1] = x16, wide
    gin = g_z
    for j in range(n):
        d_inner = (times(wide, down[j]) * slope_ref[j]).astype(BF16)
        dbias_ref[j : j + 1, :] = jnp.sum(d_inner.astype(F32), axis=0, keepdims=True)
        stash[j % groups][2 + held + j // groups] = d_inner
        gin = gin + times_t(d_inner, up[j])
    gin_ref[...] = gin


def weight_grad(kind, refs, i, held):
    total = None
    for ref in refs:
        if kind == "d":
            part = mm_tn(ref[1], ref[2 + i])
        elif kind == "u":
            part = mm_tn(ref[0], ref[2 + held + i])
        else:
            both = ref[2 + i]
            part = mm_tn(ref[0], both)
            tail = mm_tn(ref[1], both[:, 512:])
            own = lax.broadcasted_iota(jnp.int32, (1, 256), 1) < 64
            part = jnp.concatenate([part[:, :512], jnp.where(own, part[:, 512:], tail)], axis=1)
        total = part if total is None else total + part
    return total.astype(BF16)


def grad_kernel(kinds, held, *refs):
    outs = refs[-5:]
    s_ref, t_ref, u_ref, va_ref, vb_ref = outs
    for m, (kind, at) in enumerate(kinds):
        g = weight_grad(kind, [refs[i] for i in at], 1, held)
        half = g.shape[0] // 2
        u_ref[m], v = g[:half], g[half:]
        if len(kinds) == 1:
            va_ref[...], vb_ref[...] = v[:, : v.shape[1] // 2], v[:, v.shape[1] // 2 :]
        elif m == 0:
            va_ref[...] = v
        else:
            vb_ref[...] = v
        g = weight_grad(kind, [refs[i] for i in at], 0, held)
        s_ref[m], t_ref[m] = g[:half], g[half:]


def grad_wide_kernel(kinds, held, *refs):
    keep_ref, y_ref, x_ref = refs[-3:]
    for m, (kind, at) in enumerate(kinds):
        for x in range(2):
            g = weight_grad(kind, [refs[i] for i in at], x, held)
            half = g.shape[0] // 2
            if m == 0:
                keep_ref[x], y_ref[x] = g[:half], g[half:]
            else:
                for y in range(2):
                    out = keep_ref.at[2 + y] if x == 0 else x_ref.at[y]
                    out[...] = g[y * half : (y + 1) * half]


def close_wide_kernel(keep_ref, y_ref, x_ref, out_ref):
    rows = keep_ref.shape[1] // 4
    for b in range(4):
        for z in range(4):
            at = slice(z * rows, (z + 1) * rows)
            other = y_ref[b, at] if b < 2 else x_ref[b - 2, at]
            out_ref[z, b] = (keep_ref[b, at].astype(F32) + other.astype(F32)).astype(BF16)


def grad_plain_kernel(kinds, held, *refs):
    for m, (kind, at) in enumerate(kinds):
        for i in range(held):
            refs[len(refs) - len(kinds) + m][i] = weight_grad(kind, [refs[k] for k in at], i, held)


def bump_kernel(t_ref, u_ref, a_ref, b_ref, t_out, u_out):
    cut, cols, last = a_ref.shape[1], t_ref.shape[2], u_ref.shape[0] - 1
    t_out[...] = t_ref[...]
    u_out[...] = u_ref[...]
    t_out[0, :, :cut] = (t_ref[0, :, :cut].astype(F32) + a_ref[...].astype(F32)).astype(BF16)
    u_out[last, :, cols - cut :] = (u_ref[last, :, cols - cut :].astype(F32) + b_ref[...].astype(F32)).astype(BF16)


def close_kernel(s_ref, t_ref, u_ref, out_ref):
    n, rows = s_ref.shape[0], s_ref.shape[1] // 4
    for m in range(n):
        for z in range(4):
            at = slice(z * rows, (z + 1) * rows)
            out_ref[z, m] = (s_ref[m, at].astype(F32) + t_ref[m, at].astype(F32) + u_ref[m, at].astype(F32)).astype(BF16)


def small(kernel, args, outs, micros, limit=24, after=()):
    vmem, n_in = pl.BlockSpec(memory_space=pltpu.VMEM), len(args)

    def body(*refs):
        kernel(*refs[:n_in], *refs[n_in + len(after) :])

    return pl.pallas_call(
        body,
        in_specs=[vmem] * n_in + [pl.BlockSpec(memory_space=pl.ANY)] * len(after),
        out_specs=tuple([vmem] * len(outs)),
        out_shape=tuple(outs),
        cost_estimate=work(micros),
        compiler_params=pltpu.CompilerParams(vmem_limit_bytes=limit * MIB),
    )(*args, *after)


def several(specs, micros):
    def body(*refs):
        at, out = 0, sum(len(s[1]) for s in specs)
        for kernel, args, outs in specs:
            kernel(*refs[at : at + len(args)], *refs[out : out + len(outs)])
            at, out = at + len(args), out + len(outs)

    res = list(small(body, [a for s in specs for a in s[1]], [o for s in specs for o in s[2]], micros, 40))
    return [[res.pop(0) for _ in s[2]] for s in specs]


def flat(ref):
    k, _, r, c = ref.shape
    return ref[...].reshape(k * r, c)


def times(x, refs):
    total, at = None, 0
    for ref in refs:
        w = flat(ref)
        part = mm(x[:, at : at + w.shape[0]], w)
        total = part if total is None else total + part
        at += w.shape[0]
    return total


def times_t(x, refs, start=0, stop=None):
    return jnp.concatenate([mm_nt(x, flat(ref)[:, start:stop]) for ref in refs], axis=1)


def times_from(x, refs, start):
    total, at = None, 0
    for ref in refs:
        w = flat(ref)[:, start:]
        part = mm(x[:, at : at + w.shape[0]], w)
        total = part if total is None else total + part
        at += w.shape[0]
    return total


def split(refs, n):
    size = len(refs) // n
    return [refs[i * size : (i + 1) * size] for i in range(n)]


MIB = 1024 * 1024
SCALE = 0.2


def work(micros):
    return pl.CostEstimate(flops=int(micros * SCALE * 1.1e9), bytes_accessed=1024, transcendentals=0)


def call(kernel, args, weights, outs, cost, vmem, after=(), scratch=()):
    chunks = [c for piece in weights for c in piece]
    n_in, waits = len(args) + len(chunks), len(after)

    def body(*refs):
        kernel(*refs[:n_in], *refs[n_in + waits :])

    once = pl.Buffered(buffer_count=1)

    def whole(a):
        return pl.BlockSpec(a.shape, lambda i, nd=len(a.shape): (0,) * nd, pipeline_mode=once)

    def picked(a, m):
        k, _, r, c = a.shape
        return pl.BlockSpec((k, 1, r, c), lambda i: (0, m, 0, 0), pipeline_mode=once)

    return pl.pallas_call(
        body,
        grid=(1,),
        out_shape=tuple(outs),
        scratch_shapes=list(scratch),
        in_specs=[whole(a) for a in args] + [picked(a, m) for a, m in chunks]
        + [pl.BlockSpec(memory_space=pl.ANY)] * waits,
        out_specs=tuple(whole(o) for o in outs),
        compiler_params=pltpu.CompilerParams(vmem_limit_bytes=vmem * MIB),
        cost_estimate=cost,
    )(*args, *[a for a, m in chunks], *after)


def shape(dims, kind=F32):
    return jax.ShapeDtypeStruct(dims, kind)


def dims_of(piece):
    return [a.shape[0] * a.shape[2] for a, m in piece], piece[0][0].shape[3]


def count(w):
    return len(w), sum(len(p) for p in w)


def att_forward(x, mask, bias, vec, w, hn):
    (n, nw), (rows, width) = count(w), x.shape
    outs = [shape((rows, width)), shape((rows, width)), shape((rows, 128)), shape((n, rows, 768), BF16), shape((n, rows, 256), BF16)]
    return call(functools.partial(att_fwd_kernel, n, nw, hn), [x, mask, bias, vec], w, outs, work(4 + rows / 50), 30)


def att_backward(g, x, mask, vec, kept, w, hn, groups, after=()):
    (n, nw), (rows, width) = count(w), x.shape
    outs = [shape((rows, width)), shape((8, width)), shape((2, width))] + [shape((2 + n // groups, rows, width), BF16)] * groups
    res = call(functools.partial(att_bwd_kernel, n, nw, hn), [g, x, mask, vec] + list(kept), w, outs, work(4 + rows / 26), 30, after)
    return res[0], res[1], res[2], res[3:]


def ffn_both(x, cot, bias, vec, up, down, groups, after=()):
    (n, nw), (rows, width), f = count(up), x.shape, dims_of(up[0])[1]
    outs = [shape((rows, width)), shape((rows, width)), shape((8, width)), shape((n, f))]
    outs += [shape((2 + 2 * n // groups, rows, width), BF16)] * groups
    scratch = [pltpu.VMEM((n, rows, f), F32)]
    res = call(functools.partial(ffn_kernel, n, nw), [x, cot, bias, vec], up + down, outs, work(7 + rows / 50), 38, after, scratch)
    return res[0], res[1], res[2], res[3], res[4:]


def weight_kinds(items):
    stashes = []
    kinds = []
    for kind, arrays in items:
        at = []
        for array in arrays:
            same = [i for i, s in enumerate(stashes) if s is array]
            at.append(same[0] if same else len(stashes))
            stashes += [] if same else [array]
        kinds.append((kind, tuple(at)))
    return stashes, tuple(kinds)


def make_local(mesh):
    n_t = mesh.shape["tensor"]
    net = (Grid if (mesh.shape["dp"], n_t) == (8, 4) else Plain)(mesh)

    def local(
        lang_in, visn_in, word_len, lang_cot, visn_cot, att_in, att_out, ffn_up, ffn_down, vectors, ffn_bias1,
        att_in_m, att_in_v, att_out_m, att_out_v, ffn_up_m, ffn_up_v, ffn_down_m, ffn_down_v,
        vectors_m, vectors_v, bias1_m, bias1_v,
    ):
        width = lang_in.shape[1]
        rows = att_in.shape[1]
        cols = att_in.shape[3]
        ff = ffn_up.shape[2]
        heads_here = cols // HD
        items = word_len.shape[0]
        usable = jnp.arange(LW, dtype=jnp.int32)[None, :] < word_len[:, None]

        shards = {}
        for b in range(3):
            shards["a%d" % b] = jnp.concatenate(
                [att_in[b].astype(BF16).reshape(rows, 3 * cols), att_out[b].astype(BF16).T], axis=1
            )
        for i in range(2):
            shards["u%d" % i] = ffn_up[i].astype(BF16)
            shards["d%d" % i] = ffn_down[i].astype(BF16).T

        index_of = (net.row_blocks()[:, None] * rows + jnp.arange(rows, dtype=jnp.int32)[None, :]).reshape(-1)
        turn = (jnp.arange(width, dtype=jnp.int32)[:, None] == index_of[None, :])
        turn16, turn32 = turn.astype(BF16), turn.astype(F32)

        def to_rel(value):
            return mm(value, turn16).astype(BF16)

        def to_abs(value):
            return lax.dot_general(value, turn32, (((1,), (1,)), ((), ())), precision=HIGHEST)

        pieces = jnp.stack([net.piece_at(j) for j in range(n_t)])
        chosen = pieces[:, None] == jnp.arange(n_t, dtype=jnp.int32)[None, :]
        column = (pieces[:, None] * cols + jnp.arange(cols, dtype=jnp.int32)[None, :]).reshape(-1)
        turn_heads = (jnp.arange(width, dtype=jnp.int32)[:, None] == column[None, :]).astype(F32)

        def by_piece(value):
            return jnp.sum(jnp.where(chosen[None, :, :, None], value[:, None], 0.0), axis=2)

        vec = jnp.dot(vectors, turn32, precision=HIGHEST)
        vec_heads = jnp.dot(vectors, turn_heads, precision=HIGHEST)
        bias_ff = by_piece(ffn_bias1.reshape(2, n_t, ff))
        qv = [vec_heads[5 * b : 5 * b + 2] for b in range(3)]

        def rows3(row):
            return vec[row : row + 3]

        n_lang, n_visn = lang_in.shape[0], visn_in.shape[0]
        slots, regions = n_lang // items, n_visn // items
        item = jnp.concatenate([jnp.arange(n_lang) // slots, jnp.arange(n_visn) // regions])
        is_lang = jnp.arange(n_lang + n_visn) < n_lang
        seen = jnp.concatenate([usable.reshape(-1), jnp.ones((n_visn,), bool)])
        same = (item[:, None] == item[None, :]) & seen[None, :]
        mask0 = (same & (is_lang[:, None] != is_lang[None, :])).astype(F32)
        mask1 = same[:n_lang, :n_lang].astype(F32)
        mask2 = same[n_lang:, n_lang:].astype(F32)

        x0 = to_rel(jnp.concatenate([lang_in, visn_in], axis=0)).astype(F32)
        near, full = net.first(shards)
        later = tie({k: v for k, v in shards.items() if k != "a0"}, shards["a0"])
        pair3 = net.begin_late(("u1", "d1"), later)
        later = tie(later, near)
        pair1 = net.begin(("a1", "a2"), later, ())
        both1, *kept0 = att_forward(x0, mask0, qv[0], rows3(2), full["a0"], heads_here)
        pair3 = net.gather_late(pair3, both1)
        full.update(net.complete(pair1, both1))
        pair2 = net.begin(("u0", "d0"), later, net.begun(pair1))
        lang1, visn1 = both1[:n_lang], both1[n_lang:]
        lang2, *kept1 = att_forward(lang1, mask1, qv[1], rows3(7), full["a1"], heads_here)
        visn2, *kept2 = att_forward(visn1, mask2, qv[2], rows3(12), full["a2"], heads_here)
        full.update(net.complete(pair2, (lang2, visn2)))
        pair3 = net.complete_late(pair3, full["d0"][-1][-1][0])
        groups = net.groups
        lang_out, g_lang, sums15, bias_lang, stash = ffn_both(lang2, to_rel(lang_cot), bias_ff[0], rows3(15), full["u0"], full["d0"], groups)
        rows_f0 = net.swap_out(stash)
        g_lang, sums7, bias1, stash = att_backward(g_lang, lang1, mask1, rows3(7), kept1, full["a1"], heads_here, groups)
        rows_a1 = net.swap_out(stash)
        lang_out = to_abs(lang_out)
        part0 = net.fold_wide([("d", rows_f0), ("u", rows_f0)], [sums7, lang_out])
        full.update(net.swap_late(pair3, net.gate(part0)))
        first = ffn_both(visn2, to_rel(visn_cot), bias_ff[1], rows3(18), full["u1"], full["d1"], groups, net.gate(part0))
        visn_out, g_visn, sums18, bias_visn, stash = tie(first, net.landed(part0))
        rows_f1 = net.swap_out(stash)
        part0 = net.merge(part0, sums18)
        held0 = net.over_z(part0)
        part1 = net.send(net.fold([("d", rows_f1), ("u", rows_f1)], net.gate(part0)))
        first = att_backward(g_visn, visn1, mask2, rows3(12), kept2, full["a2"], heads_here, groups, net.gate(part1))
        (part1,) = net.bump(part1, after=first[1])
        g_visn, sums12, bias2, stash = tie(first, net.gate(part1))
        part1 = net.go(part1)
        rows_a2 = net.swap_out(stash)
        part2 = net.send(net.fold([("a", rows_a1), ("a", rows_a2)], net.gate(part1)))
        first = att_backward(
            jnp.concatenate([g_lang, g_visn], axis=0), x0, mask0, rows3(2), kept0, full["a0"], heads_here, groups, net.gate(part2)
        )
        part1, part2 = net.merge_and_bump(part1, part2, after=first[1])
        g_both, sums2, bias0, stash = tie(first, net.gate(part1))
        part2 = net.go(part2)
        rows_a0 = net.swap_out(stash)
        held1 = net.over_z(part1)
        part3 = net.send(net.fold([("a", rows_a0)], net.gate(part2)))
        blank = jnp.zeros((2, width), F32)
        by_rows = to_abs(jnp.concatenate([blank, sums2[:3], blank, sums7[:3], blank, sums12[:3], sums15[:3], sums18[:3]], axis=0))
        by_heads = lax.dot_general(
            jnp.concatenate([bias0, bias1, bias2], axis=0), turn_heads, (((1,), (1,)), ((), ())), precision=HIGHEST
        )
        lang_grad, visn_grad, visn_out = to_abs(g_both[:n_lang]), to_abs(g_both[n_lang:]), to_abs(visn_out)

        whole = []
        for b in range(3):
            whole += [by_heads[2 * b : 2 * b + 2], by_rows[5 * b + 2 : 5 * b + 5]]
        by_rows = jnp.concatenate(whole + [by_rows[15:]], axis=0)
        bias_all = by_piece(jnp.stack([bias_lang, bias_visn]))
        sums = net.first_totals(tie(jnp.concatenate([by_rows, bias_all.reshape(-1, width)], axis=0), net.gate(part3)))
        part2, part3 = net.merge_and_bump(part2, part3, after=listed(sums, held0, lang_grad, visn_grad, visn_out))
        part3 = net.go(part3)
        held2 = net.over_z(part2)
        share0, share1, share2 = net.rest(held0), net.rest(held1), net.rest(held2)

        t_in, t_in_m, t_in_v = (jnp.transpose(k, (0, 2, 1, 3)) for k in (att_in, att_in_m, att_in_v))
        up_all = (ffn_up, ffn_up_m, ffn_up_v)
        down_all = [jnp.transpose(k, (0, 2, 1)) for k in (ffn_down, ffn_down_m, ffn_down_v)]
        ffn_new = adam_call(adam_ffn_kernel, (0,), share0[1::-1], [up_all, down_all], None)
        ffn_new = adam_call(adam_ffn_kernel, (1,), share1[1::-1], [up_all, down_all], ffn_new)
        sums = net.next_total(sums, "x", net.gate(part2))
        part3 = net.merge(part3, [ffn_new[0], sums])
        sums = net.next_total(sums, "y", net.gate(part3))
        vector_grad, bias1_grad = sums[:21], sums[21:].reshape(ffn_bias1.shape)

        att_all = [(t_in, t_in_m, t_in_v), (att_out, att_out_m, att_out_v)]
        att_new = adam_call(adam_att_kernel, (1,), share2[:1], att_all, None)
        att_new = adam_call(adam_att_kernel, (2,), share2[1:], att_all, att_new)
        share3 = net.rest(net.over_z(part3, att_new[0]))
        att_new = adam_call(adam_att_kernel, (0,), share3, att_all, att_new)
        in_new = [jnp.transpose(k, (0, 2, 1, 3)) for k in att_new[:5]]

        result = [lang_out, visn_out, lang_grad, visn_grad] + in_new + list(att_new[5:]) + list(ffn_new[:5]) + [jnp.transpose(k, (0, 2, 1)) for k in ffn_new[5:]]
        for share, weight, first, second, rate in (
            (vector_grad, vectors, vectors_m, vectors_v, rate_vector),
            (bias1_grad, ffn_bias1, bias1_m, bias1_v, rate_bias),
        ):
            m_new, v_new, w_new = adam_step(weight, share, first, second, rate)
            result += [share, m_new, v_new, w_new]
        return tuple(result)

    return local


def solution(mesh):
    rows = P(("dp", "tensor"), None)
    w_in, w_out, w_up, w_down = P(None, "dp", None, "tensor"), P(None, "tensor", "dp"), P(None, "dp", "tensor"), P(None, "tensor", "dp")
    return jax.shard_map(
        make_local(mesh),
        mesh=mesh,
        in_specs=(rows, rows, P(("dp", "tensor")), rows, rows, w_in, w_out, w_up, w_down, P(), P())
        + (w_in,) * 2 + (w_out,) * 2 + (w_up,) * 2 + (w_down,) * 2 + (P(),) * 4,
        out_specs=(rows,) * 4 + (w_in,) * 5 + (w_out,) * 5 + (w_up,) * 5 + (w_down,) * 5 + (P(),) * 8,
        check_vma=False,
    )
```

```python
import functools

import jax
import jax.numpy as jnp
from jax import lax
from jax.experimental import pallas as pl
from jax.experimental.pallas import tpu as pltpu
from jax.sharding import PartitionSpec as P

HD = 64
LW = 20
STEP = 10

lnorm_eps = 1e-12
decay_one = 0.5
decay_two = 0.5
adam_eps = 1e-08
weight_decay = 0.01
rate_in = 0.03
rate_out = 0.1
rate_up = 0.03
rate_down = 0.015
rate_vector = 0.2
rate_bias = 0.2

F32 = jnp.float32
BF16 = jnp.bfloat16
HIGHEST = lax.Precision.HIGHEST

def tie(value, after):
    return lax.optimization_barrier((value, after))[0]


def listed(*values):
    return jax.tree.leaves(values)


class Plain:
    def __init__(self, mesh):
        self.n_dp, self.n_t = mesh.shape["dp"], mesh.shape["tensor"]
        self.groups = 1

    def row_blocks(self):
        return jnp.arange(self.n_dp, dtype=jnp.int32)

    def piece_at(self, j):
        return jnp.int32(j)

    def gather(self, shard):
        whole = lax.all_gather(shard, "dp", axis=0)[:, None]
        for_all = lax.all_gather(whole, "tensor", axis=0)
        return [[(for_all[j], 0)] for j in range(self.n_t)]

    def first(self, shards):
        return (), {"a0": self.gather(shards["a0"])}

    def begin(self, pair, shards, after):
        return {name: self.gather(shards[name]) for name in pair}

    def begin_late(self, pair, shards):
        return self.begin(pair, shards, ())

    def gather_late(self, state, after):
        return state

    def complete_late(self, state, after):
        return state

    def swap_late(self, state, after):
        return state

    def begun(self, state):
        return ()

    def complete(self, state, after):
        return state

    def swap_out(self, stash):
        return list(stash)

    def fold(self, items, after=()):
        stashes, kinds = weight_kinds(items)
        outs = [shape((self.n_t, stashes[0].shape[2], stashes[0].shape[2]), BF16)] * len(items)
        return small(functools.partial(grad_plain_kernel, kinds, self.n_t), stashes, outs, 8, 40, after)

    def fold_wide(self, items, after=()):
        return self.fold(items, after)

    def send(self, state, after=()):
        return state

    def bump(self, *states, after=()):
        return list(states)

    def merge_and_bump(self, state, *others, after=()):
        return [state, *others]

    def go(self, state, after=()):
        return state

    def landed(self, state):
        return ()

    def merge(self, state, after=()):
        return state

    def rest(self, shares):
        return shares

    def over_z(self, state, after=()):
        out = []
        for full in state:
            mine = lax.psum_scatter(full, "tensor", scatter_dimension=0)
            out.append(lax.psum_scatter(mine, "dp", scatter_dimension=0, tiled=True))
        return out

    def gate(self, state):
        return []

    def first_totals(self, value):
        return lax.psum(value, ("dp", "tensor"))

    def next_total(self, value, axis, after):
        return value


class Grid:
    def __init__(self, mesh):
        self.n_dp, self.n_t = mesh.shape["dp"], mesh.shape["tensor"]
        self.groups = 2
        self.z_groups = [[z * 2 + y for z in range(4)] for y in range(2)]

    def row_blocks(self):
        y = lax.axis_index("dp") % 2
        return jnp.stack([2 * z + (y ^ k) for k in range(2) for z in range(4)])

    def piece_at(self, j):
        return lax.axis_index("tensor") ^ j

    def swap(self, value, axis, mask):
        size = self.n_dp if axis == "dp" else self.n_t
        return lax.ppermute(value, axis, [(i, i ^ mask) for i in range(size)])

    def over_x(self, value):
        return self.swap(value, "tensor", 2)

    def over_core(self, value):
        return self.swap(value, "tensor", 1)

    def over_y(self, value):
        return self.swap(value, "dp", 1)

    def z_gather(self, value):
        z = lax.axis_index("dp") // 2
        out = jnp.zeros((4,) + value.shape, value.dtype)
        out = lax.dynamic_update_slice_in_dim(out, value[None], z, 0)
        near = self.swap(value, "dp", 2)
        out = lax.dynamic_update_slice_in_dim(out, near[None], z ^ 1, 0)
        for m in range(2, 4):
            out = lax.dynamic_update_slice_in_dim(out, self.swap(value, "dp", 2 * m)[None], z ^ m, 0)
        return out, near

    def z_scatter(self, value, after):
        z = lax.axis_index("dp") // 2
        total = lax.dynamic_index_in_dim(value, z, 0, keepdims=False).astype(F32)
        parts = [lax.dynamic_index_in_dim(value, z ^ m, 0, keepdims=False) for m in range(1, 4)]
        for part in tie([self.swap(part, "dp", 2 * m) for m, part in enumerate(parts, 1)], after):
            total = total + part.astype(F32)
        return total.astype(BF16)

    def first(self, shards):
        s, near = self.z_gather(shards["a0"][None])
        u, t = self.over_x(s), self.over_y(s)
        half = s.shape[-1] // 2
        v = jnp.concatenate([self.over_x(t[..., :half]), self.over_y(u[..., half:])], axis=-1)
        mine = (s, t, u, v)
        other = [self.over_core(k) for k in mine]
        return near, {"a0": [[(k[0], 0), (k[1], 0)] if j < 2 else [(k[2], 0), (k[3], 0)] for j, k in enumerate((mine, other, mine, other))]}

    def begin(self, pair, shards, after):
        s = lax.all_gather(jnp.stack([shards[n] for n in pair]), "dp", axis=0, axis_index_groups=self.z_groups)
        s = tie(s, after)
        return pair, s, self.over_x(s), self.over_y(s)

    def begin_late(self, pair, shards):
        first, second = shards[pair[0]], shards[pair[1]]
        blocks = jnp.stack([first, self.over_x(first), second, self.over_y(second)])
        return pair, blocks

    def gather_late(self, state, after):
        pair, blocks = state
        return pair, lax.all_gather(tie(blocks, after), "dp", axis=0, axis_index_groups=self.z_groups)

    def complete_late(self, state, after):
        pair, held = state
        cut = tie(held, after)
        return pair, held, self.over_y(cut[:, :2]), self.over_x(cut[:, 2:])

    def swap_late(self, state, after):
        pair, mine = state[0], state[1:]
        other = [self.over_core(mine[0])] + [self.over_core(k) for k in tie(mine[1:], after)]
        out = {pair[0]: [], pair[1]: []}
        for x in range(2):
            for k in (mine, other):
                out[pair[0]].append([(k[0], x), (k[1], x)])
                out[pair[1]].append([(k[2 * x], 2 - 2 * x), (k[2 * x], 3 - 2 * x)])
        return out

    def begun(self, state):
        return state[3:]

    def complete(self, state, after):
        pair, s, u, t = state
        cut_t, cut_u = tie((t, u), after)
        v0, v1 = self.over_x(cut_t[:, 0:1]), self.over_y(cut_u[:, 1:2])
        mine = (s, t, u, v0, v1)
        other = [self.over_core(k) for k in mine]
        out = {}
        for m, name in enumerate(pair):
            out[name] = [
                [(k[0], m), (k[1], m)] if j < 2 else [(k[2], m), (k[3 + m], 0)] for j, k in enumerate((mine, other, mine, other))
            ]
        return out

    def swap_out(self, stash):
        keep, send = stash
        return [keep, self.over_core(send)]

    def fold(self, items, after=()):
        stashes, kinds = weight_kinds(items)
        n, cols = len(items), stashes[0].shape[2]
        half = cols // 2
        cut = cols if n == 2 else cols // 2
        outs = (shape((n, half, cols), BF16),) * 3 + (shape((half, cut), BF16),) * 2
        s, t, u, va, vb = small(functools.partial(grad_kernel, kinds, 2), stashes, outs, 3, 30, after)
        return s, t, u, va, vb

    def fold_wide(self, items, after=()):
        stashes, kinds = weight_kinds(items)
        half, cols = stashes[0].shape[2] // 2, stashes[0].shape[2]
        outs = [shape((n, half, cols), BF16) for n in (4, 2, 2)]
        keep, ty, tx = small(functools.partial(grad_wide_kernel, kinds, 2), stashes, outs, 3, 30, after)
        return keep, self.over_y(ty), self.over_x(tx), None

    def send(self, state, after=()):
        s, t, u, va, vb = state
        va, vb = tie((va, vb), after)
        return s, t, u, self.over_x(va), self.over_y(vb)

    def bump_spec(self, state, after=()):
        s, t, u, ra, rb = state
        t, u = tie((t, u), after)
        return bump_kernel, [t, u, ra, rb], [shape(t.shape, BF16), shape(u.shape, BF16)]

    def bump(self, *states, after=()):
        done = several([self.bump_spec(k, after) for k in states], 1.5 * len(states))
        return [(k[0], t, u) for k, (t, u) in zip(states, done)]

    def merge_spec(self, state, after=()):
        s, rt, ru, wide = state
        n, half, cols = s.shape
        if wide is None:
            return close_wide_kernel, [tie(s, after), rt, ru], [shape((4, 4, half // 4, cols), BF16)]
        return close_kernel, [tie(s, after), rt, ru], [shape((4, n, half // 4, cols), BF16)]

    def merge_and_bump(self, state, *others, after=()):
        done = several([self.merge_spec(state, after)] + [self.bump_spec(k, after) for k in others], 1.5 + 1.5 * len(others))
        return [done[0][0]] + [(k[0], t, u) for k, (t, u) in zip(others, done[1:])]

    def go(self, state, after=()):
        s, t, u = state
        cut_t, cut_u = tie((t, u), after)
        return s, self.over_y(cut_t), self.over_x(cut_u), t

    def landed(self, state):
        return state[1:3]

    def merge(self, state, after=()):
        return several([self.merge_spec(state, after)], 1.5)[0][0]

    def over_z(self, both, after=()):
        if both.shape[1] == 1:
            return self.z_scatter(both, after)
        return lax.psum_scatter(both, "dp", scatter_dimension=0, axis_index_groups=self.z_groups)

    def rest(self, held):
        if held.shape[0] == 4:
            return [held[0] + self.over_x(held[1]), held[2] + self.over_y(held[3])]
        return [held[i] for i in range(held.shape[0])]

    def gate(self, state):
        if not isinstance(state, tuple):
            return [state]
        if len(state) == 4:
            return [state[0] if state[3] is None else state[3]]
        return [state[1] if len(state) == 3 else state[0]]

    def first_totals(self, value):
        for axis, mask in (("tensor", 1), ("dp", 2), ("dp", 4)):
            value = value + self.swap(value, axis, mask)
        return value

    def next_total(self, value, axis, after):
        value = tie(value, after)
        return value + (self.over_x(value) if axis == "x" else self.over_y(value))


def adam_step(weight, gradient, first, second, rate):
    first_new = decay_one * first + (1.0 - decay_one) * gradient
    second_new = decay_two * second + (1.0 - decay_two) * gradient * gradient
    fix_one = 1.0 - decay_one**STEP
    fix_two = 1.0 - decay_two**STEP
    ratio = first_new / fix_one / (jnp.sqrt(second_new / fix_two) + adam_eps)
    return (first_new, second_new, weight - rate * (ratio + weight_decay * weight))


def mm(left, right):
    return jnp.dot(left, right, preferred_element_type=F32)


def mm_nt(left, right):
    return lax.dot_general(left, right, (((1,), (1,)), ((), ())), preferred_element_type=F32)


def mm_tn(left, right):
    return lax.dot_general(left, right, (((0,), (0,)), ((), ())), preferred_element_type=F32)


def normed(z, gain, shift):
    centered = z - jnp.mean(z, axis=-1, keepdims=True)
    scale = lax.rsqrt(jnp.mean(centered * centered, axis=-1, keepdims=True) + lnorm_eps)
    xhat = centered * scale
    return xhat * gain + shift, xhat, scale


def norm_back(g, xhat, scale, gain, sums_ref):
    gg = g * gain
    g_z = (gg - jnp.mean(gg, axis=-1, keepdims=True) - xhat * jnp.mean(gg * xhat, axis=-1, keepdims=True)) * scale
    sums_ref[...] = jnp.zeros(sums_ref.shape, F32)
    sums_ref[0:1, :] = jnp.sum(g_z, axis=0, keepdims=True)
    sums_ref[1:2, :] = jnp.sum(g * xhat, axis=0, keepdims=True)
    sums_ref[2:3, :] = jnp.sum(g, axis=0, keepdims=True)
    return g_z


def put_adam(refs, at, gradient, rate):
    w_ref, m_ref, v_ref, g_out, m_out, v_out, w_out, copy_out = refs
    m_new, v_new, w_new = adam_step(w_ref[at], gradient, m_ref[at], v_ref[at], rate)
    g_out[at], m_out[at], v_out[at], w_out[at] = gradient, m_new, v_new, w_new
    copy_out[at] = w_new.astype(BF16)


def adam_ffn_kernel(ins, outs, up_ref, down_ref):
    put_adam(ins[:3] + outs[:5], 0, up_ref[...].astype(F32), rate_up)
    put_adam(ins[3:] + outs[5:], 0, down_ref[...].astype(F32), rate_down)


def adam_att_kernel(ins, outs, share_ref):
    g = share_ref[...].astype(F32)
    cols = ins[0].shape[3]
    for i in range(3):
        put_adam(ins[:3] + outs[:5], (0, i), g[:, i * cols : (i + 1) * cols], rate_in)
    put_adam(ins[3:] + outs[5:], 0, g[:, 3 * cols :].T, rate_out)


def adam_call(kernel, at, shares, groups, earlier):
    flat_in = [a for g in groups for a in g]

    def one(a):
        return pl.BlockSpec((1,) + a.shape[1:], lambda i: at + (0,) * (len(a.shape) - 1))

    outs = []
    for g in groups:
        outs += [shape(g[0].shape)] * 4 + [shape(g[0].shape, BF16)]
    n, n_in, old = len(shares), len(flat_in), list(earlier or ())

    def body(*refs):
        kernel(refs[n : n + n_in], refs[n + n_in + len(old) :], *refs[:n])

    return pl.pallas_call(
        body,
        grid=(1,),
        in_specs=[pl.BlockSpec(a.shape, lambda i: (0, 0)) for a in shares] + [one(a) for a in flat_in] + [pl.BlockSpec(memory_space=pl.ANY)] * len(old),
        out_specs=tuple(one(o) for o in outs),
        out_shape=tuple(outs),
        input_output_aliases={n + n_in + i: i for i in range(len(old))},
        cost_estimate=work(3),
        compiler_params=pltpu.CompilerParams(vmem_limit_bytes=24 * MIB),
    )(*shares, *flat_in, *old)


def head_lanes(hn, width):
    lane = lax.broadcasted_iota(jnp.int32, (1, width), 1) // HD
    return [lane == h for h in range(hn)]


def stacked(value, lanes):
    return jnp.concatenate([jnp.where(m, value, 0.0) for m in lanes], axis=0).astype(BF16)


def gathered(value, lanes):
    rows = value.shape[0] // len(lanes)
    parts = [jnp.where(m, value[h * rows : (h + 1) * rows], 0.0) for h, m in enumerate(lanes)]
    return sum(parts[1:], parts[0])


def probabilities(q_rows, k, mask):
    rows = mask.shape[0]
    s = mm_nt(q_rows, k).reshape(-1, rows, rows) * HD ** (-0.5)
    s = jnp.where(mask[None] > 0, s, -1e30)
    e = jnp.exp(s - jnp.max(s, axis=-1, keepdims=True))
    return (e / jnp.sum(e, axis=-1, keepdims=True)).reshape(-1, rows)


def att_fwd_kernel(n, nw, hn, x_ref, mask_ref, bias_ref, vec_ref, *refs):
    w, (out_ref, xhat_ref, scale_ref, qkv_ref, mix_ref) = split(refs[:nw], n), refs[nw:]
    c, lanes = hn * HD, head_lanes(hn, 256)
    x = x_ref[...]
    x16 = x.astype(BF16)
    z = x + vec_ref[0:1, :]
    for j in range(n):
        blank = jnp.zeros((1, c), F32)
        bias = jnp.concatenate([bias_ref[0:1, j * c : (j + 1) * c], blank, bias_ref[1:2, j * c : (j + 1) * c], blank], axis=1)
        qkv = times(x16, w[j]) + bias
        k = pltpu.roll(qkv[:, c - 64 : c + 192], 192, 1).astype(BF16)
        q, v = qkv[:, :256].astype(BF16), qkv[:, 2 * c : 2 * c + 256].astype(BF16)
        qkv_ref[j, :, :256], qkv_ref[j, :, 256:512], qkv_ref[j, :, 512:] = q, k, v
        p = probabilities(stacked(q.astype(F32), lanes), k, mask_ref[...]).astype(BF16)
        mix = pltpu.roll(gathered(mm(p, v), lanes), 64, 1).astype(BF16)
        mix_ref[j] = mix
        z = z + times_t(mix, w[j], 3 * c - 64)
    out, xhat, scale = normed(z, vec_ref[1:2, :], vec_ref[2:3, :])
    out_ref[...] = out
    xhat_ref[...] = xhat
    scale_ref[...] = jnp.broadcast_to(scale, scale_ref.shape)


def att_bwd_kernel(n, nw, hn, g_ref, x_ref, mask_ref, vec_ref, xhat_ref, scale_ref, qkv_ref, mix_ref, *refs):
    w, (gin_ref, sums_ref, bias_ref), stash = split(refs[:nw], n), refs[nw : nw + 3], refs[nw + 3 :]
    c, lanes, groups = hn * HD, head_lanes(hn, 256), len(stash)
    g_z = norm_back(g_ref[...], xhat_ref[...], scale_ref[:, 0:1], vec_ref[1:2, :], sums_ref)
    wide, x16 = g_z.astype(BF16), x_ref[...].astype(BF16)
    for ref in stash:
        ref[0], ref[1] = x16, wide
    gin = g_z
    for j in range(n):
        q, k, v = qkv_ref[j, :, :256], qkv_ref[j, :, 256:512], qkv_ref[j, :, 512:]
        d_mix = pltpu.roll(times_from(wide, w[j], 3 * c - 64), 192, 1).astype(BF16)
        da, q = stacked(d_mix.astype(F32), lanes), stacked(q.astype(F32), lanes)
        p = probabilities(q, k, mask_ref[...])
        dv = mm_tn(p.astype(BF16), da)
        dp = mm_nt(da, v)
        ds = (p * (dp - jnp.sum(p * dp, axis=-1, keepdims=True))).astype(BF16) * HD ** (-0.5)
        dq = gathered(mm(ds, k), lanes)
        dk = pltpu.roll(mm_tn(ds, q), 64, 1)
        front = [dq[:, :128], dq[:, 128:] + dk[:, :128], dk[:, 128:], dv[:, :128]]
        d_qkv = jnp.concatenate(front + [dv[:, 128:]], axis=1).astype(BF16)
        sums = jnp.sum(d_qkv.astype(F32), axis=0, keepdims=True)
        bias_ref[0:1, j * c : (j + 1) * c] = sums[:, :c]
        bias_ref[1:2, j * c : (j + 1) * c] = sums[:, 2 * c : 3 * c]
        place = stash[j % groups].at[2 + j // groups]
        place[:, :512] = d_qkv[:, :512]
        place[:, 512:640] = d_qkv[:, 512:] + mix_ref[j, :, :128]
        place[:, 640:] = mix_ref[j, :, 128:]
        gin = gin + times_t(d_qkv, w[j], 0, 640)
    gin_ref[...] = gin


def ffn_kernel(n, nw, x_ref, cot_ref, bias_ref, vec_ref, *refs):
    up, down = split(refs[:nw], n), split(refs[nw : 2 * nw], n)
    out_ref, gin_ref, sums_ref, dbias_ref = refs[2 * nw : 2 * nw + 4]
    slope_ref, stash = refs[-1], refs[2 * nw + 4 : -1]
    groups, held = len(stash), n // len(stash)
    x = x_ref[...]
    x16 = x.astype(BF16)
    z = x + vec_ref[0:1, :]
    for j in range(n):
        inner = times(x16, up[j]) + bias_ref[j : j + 1, :]
        half = 0.5 * (1.0 + lax.erf(inner * 0.7071067811865476))
        act = (inner * half).astype(BF16)
        slope_ref[j] = half + inner * (0.3989422804014327 * jnp.exp(-0.5 * inner * inner))
        stash[j % groups][2 + j // groups] = act
        z = z + times_t(act, down[j])
    out, xhat, scale = normed(z, vec_ref[1:2, :], vec_ref[2:3, :])
    out_ref[...] = out
    g_z = norm_back(cot_ref[...].astype(F32), xhat, scale, vec_ref[1:2, :], sums_ref)
    wide = g_z.astype(BF16)
    for ref in stash:
        ref[0], ref[1] = x16, wide
    gin = g_z
    for j in range(n):
        d_inner = (times(wide, down[j]) * slope_ref[j]).astype(BF16)
        dbias_ref[j : j + 1, :] = jnp.sum(d_inner.astype(F32), axis=0, keepdims=True)
        stash[j % groups][2 + held + j // groups] = d_inner
        gin = gin + times_t(d_inner, up[j])
    gin_ref[...] = gin


def weight_grad(kind, refs, i, held):
    total = None
    for ref in refs:
        if kind == "d":
            part = mm_tn(ref[1], ref[2 + i])
        elif kind == "u":
            part = mm_tn(ref[0], ref[2 + held + i])
        else:
            both = ref[2 + i]
            part = mm_tn(ref[0], both)
            tail = mm_tn(ref[1], both[:, 512:])
            own = lax.broadcasted_iota(jnp.int32, (1, 256), 1) < 64
            part = jnp.concatenate([part[:, :512], jnp.where(own, part[:, 512:], tail)], axis=1)
        total = part if total is None else total + part
    return total.astype(BF16)


def grad_kernel(kinds, held, *refs):
    outs = refs[-5:]
    s_ref, t_ref, u_ref, va_ref, vb_ref = outs
    for m, (kind, at) in enumerate(kinds):
        g = weight_grad(kind, [refs[i] for i in at], 1, held)
        half = g.shape[0] // 2
        u_ref[m], v = g[:half], g[half:]
        if len(kinds) == 1:
            va_ref[...], vb_ref[...] = v[:, : v.shape[1] // 2], v[:, v.shape[1] // 2 :]
        elif m == 0:
            va_ref[...] = v
        else:
            vb_ref[...] = v
        g = weight_grad(kind, [refs[i] for i in at], 0, held)
        s_ref[m], t_ref[m] = g[:half], g[half:]


def grad_wide_kernel(kinds, held, *refs):
    keep_ref, y_ref, x_ref = refs[-3:]
    for m, (kind, at) in enumerate(kinds):
        for x in range(2):
            g = weight_grad(kind, [refs[i] for i in at], x, held)
            half = g.shape[0] // 2
            if m == 0:
                keep_ref[x], y_ref[x] = g[:half], g[half:]
            else:
                for y in range(2):
                    out = keep_ref.at[2 + y] if x == 0 else x_ref.at[y]
                    out[...] = g[y * half : (y + 1) * half]


def close_wide_kernel(keep_ref, y_ref, x_ref, out_ref):
    rows = keep_ref.shape[1] // 4
    for b in range(4):
        for z in range(4):
            at = slice(z * rows, (z + 1) * rows)
            other = y_ref[b, at] if b < 2 else x_ref[b - 2, at]
            out_ref[z, b] = (keep_ref[b, at].astype(F32) + other.astype(F32)).astype(BF16)


def grad_plain_kernel(kinds, held, *refs):
    for m, (kind, at) in enumerate(kinds):
        for i in range(held):
            refs[len(refs) - len(kinds) + m][i] = weight_grad(kind, [refs[k] for k in at], i, held)


def bump_kernel(t_ref, u_ref, a_ref, b_ref, t_out, u_out):
    cut, cols, last = a_ref.shape[1], t_ref.shape[2], u_ref.shape[0] - 1
    t_out[...] = t_ref[...]
    u_out[...] = u_ref[...]
    t_out[0, :, :cut] = (t_ref[0, :, :cut].astype(F32) + a_ref[...].astype(F32)).astype(BF16)
    u_out[last, :, cols - cut :] = (u_ref[last, :, cols - cut :].astype(F32) + b_ref[...].astype(F32)).astype(BF16)


def close_kernel(s_ref, t_ref, u_ref, out_ref):
    n, rows = s_ref.shape[0], s_ref.shape[1] // 4
    for m in range(n):
        for z in range(4):
            at = slice(z * rows, (z + 1) * rows)
            out_ref[z, m] = (s_ref[m, at].astype(F32) + t_ref[m, at].astype(F32) + u_ref[m, at].astype(F32)).astype(BF16)


def small(kernel, args, outs, micros, limit=24, after=()):
    vmem, n_in = pl.BlockSpec(memory_space=pltpu.VMEM), len(args)

    def body(*refs):
        kernel(*refs[:n_in], *refs[n_in + len(after) :])

    return pl.pallas_call(
        body,
        in_specs=[vmem] * n_in + [pl.BlockSpec(memory_space=pl.ANY)] * len(after),
        out_specs=tuple([vmem] * len(outs)),
        out_shape=tuple(outs),
        cost_estimate=work(micros),
        compiler_params=pltpu.CompilerParams(vmem_limit_bytes=limit * MIB),
    )(*args, *after)


def several(specs, micros):
    def body(*refs):
        at, out = 0, sum(len(s[1]) for s in specs)
        for kernel, args, outs in specs:
            kernel(*refs[at : at + len(args)], *refs[out : out + len(outs)])
            at, out = at + len(args), out + len(outs)

    res = list(small(body, [a for s in specs for a in s[1]], [o for s in specs for o in s[2]], micros, 40))
    return [[res.pop(0) for _ in s[2]] for s in specs]


def flat(ref):
    k, _, r, c = ref.shape
    return ref[...].reshape(k * r, c)


def times(x, refs):
    total, at = None, 0
    for ref in refs:
        w = flat(ref)
        part = mm(x[:, at : at + w.shape[0]], w)
        total = part if total is None else total + part
        at += w.shape[0]
    return total


def times_t(x, refs, start=0, stop=None):
    return jnp.concatenate([mm_nt(x, flat(ref)[:, start:stop]) for ref in refs], axis=1)


def times_from(x, refs, start):
    total, at = None, 0
    for ref in refs:
        w = flat(ref)[:, start:]
        part = mm(x[:, at : at + w.shape[0]], w)
        total = part if total is None else total + part
        at += w.shape[0]
    return total


def split(refs, n):
    size = len(refs) // n
    return [refs[i * size : (i + 1) * size] for i in range(n)]


MIB = 1024 * 1024
SCALE = 0.2


def work(micros):
    return pl.CostEstimate(flops=int(micros * SCALE * 1.1e9), bytes_accessed=1024, transcendentals=0)


def call(kernel, args, weights, outs, cost, vmem, after=(), scratch=()):
    chunks = [c for piece in weights for c in piece]
    n_in, waits = len(args) + len(chunks), len(after)

    def body(*refs):
        kernel(*refs[:n_in], *refs[n_in + waits :])

    once = pl.Buffered(buffer_count=1)

    def whole(a):
        return pl.BlockSpec(a.shape, lambda i, nd=len(a.shape): (0,) * nd, pipeline_mode=once)

    def picked(a, m):
        k, _, r, c = a.shape
        return pl.BlockSpec((k, 1, r, c), lambda i: (0, m, 0, 0), pipeline_mode=once)

    return pl.pallas_call(
        body,
        grid=(1,),
        out_shape=tuple(outs),
        scratch_shapes=list(scratch),
        in_specs=[whole(a) for a in args] + [picked(a, m) for a, m in chunks]
        + [pl.BlockSpec(memory_space=pl.ANY)] * waits,
        out_specs=tuple(whole(o) for o in outs),
        compiler_params=pltpu.CompilerParams(vmem_limit_bytes=vmem * MIB),
        cost_estimate=cost,
    )(*args, *[a for a, m in chunks], *after)


def shape(dims, kind=F32):
    return jax.ShapeDtypeStruct(dims, kind)


def dims_of(piece):
    return [a.shape[0] * a.shape[2] for a, m in piece], piece[0][0].shape[3]


def count(w):
    return len(w), sum(len(p) for p in w)


def att_forward(x, mask, bias, vec, w, hn):
    (n, nw), (rows, width) = count(w), x.shape
    outs = [shape((rows, width)), shape((rows, width)), shape((rows, 128)), shape((n, rows, 768), BF16), shape((n, rows, 256), BF16)]
    return call(functools.partial(att_fwd_kernel, n, nw, hn), [x, mask, bias, vec], w, outs, work(4 + rows / 50), 30)


def att_backward(g, x, mask, vec, kept, w, hn, groups, after=()):
    (n, nw), (rows, width) = count(w), x.shape
    outs = [shape((rows, width)), shape((8, width)), shape((2, width))] + [shape((2 + n // groups, rows, width), BF16)] * groups
    res = call(functools.partial(att_bwd_kernel, n, nw, hn), [g, x, mask, vec] + list(kept), w, outs, work(4 + rows / 26), 30, after)
    return res[0], res[1], res[2], res[3:]


def ffn_both(x, cot, bias, vec, up, down, groups, after=()):
    (n, nw), (rows, width), f = count(up), x.shape, dims_of(up[0])[1]
    outs = [shape((rows, width)), shape((rows, width)), shape((8, width)), shape((n, f))]
    outs += [shape((2 + 2 * n // groups, rows, width), BF16)] * groups
    scratch = [pltpu.VMEM((n, rows, f), F32)]
    res = call(functools.partial(ffn_kernel, n, nw), [x, cot, bias, vec], up + down, outs, work(7 + rows / 50), 38, after, scratch)
    return res[0], res[1], res[2], res[3], res[4:]


def weight_kinds(items):
    stashes = []
    kinds = []
    for kind, arrays in items:
        at = []
        for array in arrays:
            same = [i for i, s in enumerate(stashes) if s is array]
            at.append(same[0] if same else len(stashes))
            stashes += [] if same else [array]
        kinds.append((kind, tuple(at)))
    return stashes, tuple(kinds)


def make_local(mesh):
    n_t = mesh.shape["tensor"]
    net = (Grid if (mesh.shape["dp"], n_t) == (8, 4) else Plain)(mesh)

    def local(
        lang_in, visn_in, word_len, lang_cot, visn_cot, att_in, att_out, ffn_up, ffn_down, vectors, ffn_bias1,
        att_in_m, att_in_v, att_out_m, att_out_v, ffn_up_m, ffn_up_v, ffn_down_m, ffn_down_v,
        vectors_m, vectors_v, bias1_m, bias1_v,
    ):
        width = lang_in.shape[1]
        rows = att_in.shape[1]
        cols = att_in.shape[3]
        ff = ffn_up.shape[2]
        heads_here = cols // HD
        items = word_len.shape[0]
        usable = jnp.arange(LW, dtype=jnp.int32)[None, :] < word_len[:, None]

        shards = {}
        for b in range(3):
            shards["a%d" % b] = jnp.concatenate(
                [att_in[b].astype(BF16).reshape(rows, 3 * cols), att_out[b].astype(BF16).T], axis=1
            )
        for i in range(2):
            shards["u%d" % i] = ffn_up[i].astype(BF16)
            shards["d%d" % i] = ffn_down[i].astype(BF16).T

        index_of = (net.row_blocks()[:, None] * rows + jnp.arange(rows, dtype=jnp.int32)[None, :]).reshape(-1)
        turn = (jnp.arange(width, dtype=jnp.int32)[:, None] == index_of[None, :])
        turn16, turn32 = turn.astype(BF16), turn.astype(F32)

        def to_rel(value):
            return mm(value, turn16).astype(BF16)

        def to_abs(value):
            return lax.dot_general(value, turn32, (((1,), (1,)), ((), ())), precision=HIGHEST)

        pieces = jnp.stack([net.piece_at(j) for j in range(n_t)])
        chosen = pieces[:, None] == jnp.arange(n_t, dtype=jnp.int32)[None, :]
        column = (pieces[:, None] * cols + jnp.arange(cols, dtype=jnp.int32)[None, :]).reshape(-1)
        turn_heads = (jnp.arange(width, dtype=jnp.int32)[:, None] == column[None, :]).astype(F32)

        def by_piece(value):
            return jnp.sum(jnp.where(chosen[None, :, :, None], value[:, None], 0.0), axis=2)

        vec = jnp.dot(vectors, turn32, precision=HIGHEST)
        vec_heads = jnp.dot(vectors, turn_heads, precision=HIGHEST)
        bias_ff = by_piece(ffn_bias1.reshape(2, n_t, ff))
        qv = [vec_heads[5 * b : 5 * b + 2] for b in range(3)]

        def rows3(row):
            return vec[row : row + 3]

        n_lang, n_visn = lang_in.shape[0], visn_in.shape[0]
        slots, regions = n_lang // items, n_visn // items
        item = jnp.concatenate([jnp.arange(n_lang) // slots, jnp.arange(n_visn) // regions])
        is_lang = jnp.arange(n_lang + n_visn) < n_lang
        seen = jnp.concatenate([usable.reshape(-1), jnp.ones((n_visn,), bool)])
        same = (item[:, None] == item[None, :]) & seen[None, :]
        mask0 = (same & (is_lang[:, None] != is_lang[None, :])).astype(F32)
        mask1 = same[:n_lang, :n_lang].astype(F32)
        mask2 = same[n_lang:, n_lang:].astype(F32)

        x0 = to_rel(jnp.concatenate([lang_in, visn_in], axis=0)).astype(F32)
        near, full = net.first(shards)
        later = tie({k: v for k, v in shards.items() if k != "a0"}, shards["a0"])
        pair3 = net.begin_late(("u1", "d1"), later)
        later = tie(later, near)
        pair1 = net.begin(("a1", "a2"), later, ())
        both1, *kept0 = att_forward(x0, mask0, qv[0], rows3(2), full["a0"], heads_here)
        pair3 = net.gather_late(pair3, both1)
        full.update(net.complete(pair1, both1))
        pair2 = net.begin(("u0", "d0"), later, net.begun(pair1))
        lang1, visn1 = both1[:n_lang], both1[n_lang:]
        lang2, *kept1 = att_forward(lang1, mask1, qv[1], rows3(7), full["a1"], heads_here)
        visn2, *kept2 = att_forward(visn1, mask2, qv[2], rows3(12), full["a2"], heads_here)
        full.update(net.complete(pair2, (lang2, visn2)))
        pair3 = net.complete_late(pair3, full["d0"][-1][-1][0])
        groups = net.groups
        lang_out, g_lang, sums15, bias_lang, stash = ffn_both(lang2, to_rel(lang_cot), bias_ff[0], rows3(15), full["u0"], full["d0"], groups)
        rows_f0 = net.swap_out(stash)
        g_lang, sums7, bias1, stash = att_backward(g_lang, lang1, mask1, rows3(7), kept1, full["a1"], heads_here, groups)
        rows_a1 = net.swap_out(stash)
        part0 = net.fold_wide([("d", rows_f0), ("u", rows_f0)], [sums7])
        full.update(net.swap_late(pair3, net.gate(part0)))
        first = ffn_both(visn2, to_rel(visn_cot), bias_ff[1], rows3(18), full["u1"], full["d1"], groups, net.gate(part0))
        visn_out, g_visn, sums18, bias_visn, stash = tie(first, net.landed(part0))
        rows_f1 = net.swap_out(stash)
        lang_out, visn_out = to_abs(lang_out), to_abs(first[0])
        part0 = net.merge(part0, [sums18, lang_out, visn_out])
        held0 = net.over_z(part0)
        part1 = net.send(net.fold([("d", rows_f1), ("u", rows_f1)], net.gate(part0)))
        first = att_backward(g_visn, visn1, mask2, rows3(12), kept2, full["a2"], heads_here, groups, net.gate(part1))
        (part1,) = net.bump(part1, after=first[1])
        g_visn, sums12, bias2, stash = tie(first, net.gate(part1))
        part1 = net.go(part1)
        rows_a2 = net.swap_out(stash)
        part2 = net.send(net.fold([("a", rows_a1), ("a", rows_a2)], net.gate(part1)))
        first = att_backward(
            jnp.concatenate([g_lang, g_visn], axis=0), x0, mask0, rows3(2), kept0, full["a0"], heads_here, groups, net.gate(part2)
        )
        part1, part2 = net.merge_and_bump(part1, part2, after=first[1])
        g_both, sums2, bias0, stash = tie(first, net.gate(part1))
        part2 = net.go(part2)
        rows_a0 = net.swap_out(stash)
        held1 = net.over_z(part1)
        part3 = net.send(net.fold([("a", rows_a0)], net.gate(part2)))
        blank = jnp.zeros((2, width), F32)
        by_rows = to_abs(jnp.concatenate([blank, sums2[:3], blank, sums7[:3], blank, sums12[:3], sums15[:3], sums18[:3]], axis=0))
        by_heads = lax.dot_general(
            jnp.concatenate([bias0, bias1, bias2], axis=0), turn_heads, (((1,), (1,)), ((), ())), precision=HIGHEST
        )
        lang_grad, visn_grad = to_abs(g_both[:n_lang]), to_abs(g_both[n_lang:])

        whole = []
        for b in range(3):
            whole += [by_heads[2 * b : 2 * b + 2], by_rows[5 * b + 2 : 5 * b + 5]]
        by_rows = jnp.concatenate(whole + [by_rows[15:]], axis=0)
        bias_all = by_piece(jnp.stack([bias_lang, bias_visn]))
        sums = net.first_totals(tie(jnp.concatenate([by_rows, bias_all.reshape(-1, width)], axis=0), net.gate(part3)))
        part2, part3 = net.merge_and_bump(part2, part3, after=listed(sums, held0, lang_grad, visn_grad))
        part3 = net.go(part3)
        held2 = net.over_z(part2)
        share0, share1, share2 = net.rest(held0), net.rest(held1), net.rest(held2)

        t_in, t_in_m, t_in_v = (jnp.transpose(k, (0, 2, 1, 3)) for k in (att_in, att_in_m, att_in_v))
        up_all = (ffn_up, ffn_up_m, ffn_up_v)
        down_all = [jnp.transpose(k, (0, 2, 1)) for k in (ffn_down, ffn_down_m, ffn_down_v)]
        ffn_new = adam_call(adam_ffn_kernel, (0,), share0[1::-1], [up_all, down_all], None)
        ffn_new = adam_call(adam_ffn_kernel, (1,), share1[1::-1], [up_all, down_all], ffn_new)
        sums = net.next_total(sums, "x", net.gate(part2))
        part3 = net.merge(part3, [ffn_new[0], sums])
        sums = net.next_total(sums, "y", net.gate(part3))
        vector_grad, bias1_grad = sums[:21], sums[21:].reshape(ffn_bias1.shape)

        att_all = [(t_in, t_in_m, t_in_v), (att_out, att_out_m, att_out_v)]
        att_new = adam_call(adam_att_kernel, (1,), share2[:1], att_all, None)
        att_new = adam_call(adam_att_kernel, (2,), share2[1:], att_all, att_new)
        share3 = net.rest(net.over_z(part3, att_new[0]))
        att_new = adam_call(adam_att_kernel, (0,), share3, att_all, att_new)
        in_new = [jnp.transpose(k, (0, 2, 1, 3)) for k in att_new[:5]]

        result = [lang_out, visn_out, lang_grad, visn_grad] + in_new + list(att_new[5:]) + list(ffn_new[:5]) + [jnp.transpose(k, (0, 2, 1)) for k in ffn_new[5:]]
        for share, weight, first, second, rate in (
            (vector_grad, vectors, vectors_m, vectors_v, rate_vector),
            (bias1_grad, ffn_bias1, bias1_m, bias1_v, rate_bias),
        ):
            m_new, v_new, w_new = adam_step(weight, share, first, second, rate)
            result += [share, m_new, v_new, w_new]
        return tuple(result)

    return local


def solution(mesh):
    rows = P(("dp", "tensor"), None)
    w_in, w_out, w_up, w_down = P(None, "dp", None, "tensor"), P(None, "tensor", "dp"), P(None, "dp", "tensor"), P(None, "tensor", "dp")
    return jax.shard_map(
        make_local(mesh),
        mesh=mesh,
        in_specs=(rows, rows, P(("dp", "tensor")), rows, rows, w_in, w_out, w_up, w_down, P(), P())
        + (w_in,) * 2 + (w_out,) * 2 + (w_up,) * 2 + (w_down,) * 2 + (P(),) * 4,
        out_specs=(rows,) * 4 + (w_in,) * 5 + (w_out,) * 5 + (w_up,) * 5 + (w_down,) * 5 + (P(),) * 8,
        check_vma=False,
    )
```
